1024 devices in a mesh: mode: 32 (over y_hi, x, core), space: 32 (over z, y_lo).
Axes of the slice: x: 4, y: 8 (y_hi: 4, y_lo: 2; y = y_hi * 2 + y_lo), z: 16, core: 2. Of those that a mesh axis runs over, the one named last changes fastest.
Arguments:
- left_modes: bfloat16 [2048, 24, 4096], P('mode', None, 'space'), may hold values from -6 to 6
- right_modes: bfloat16 [2048, 24, 4096], P('mode', None, 'space'), may hold values from -6 to 6
- momenta: int32 [8, 3], replicated, may hold values from -3 to 3
- spin_perm: int32 [8, 4], replicated, may hold values from 0 to 3, each once within a row
- spin_phase: int32 [8, 4], replicated, may hold values from 0 to 3
Outputs:
- fields: float32 [64, 2048, 64], P('space', 'mode')
The draws below stay inside these ranges and needn't reach their ends.
Inputs may be any that keep to these rules, and one draw needn't show every extreme that they name: `spin_perm`: each row is a permutation of 0 to 3.
All inputs are finite; a program needn't handle non-finite values.
Results may differ from the reference program's by a relative error of at most 0.0028.
Values may be sent and summed in bfloat16 or wider, within the bound.
A program may use at most 32 MiB of HBM per device.

```python
import math
import jax
import jax.numpy as jnp
from jax import lax

MODE_DEV = 64
MODES = 2048
COMP = 24
STRUCTS = 8
CYCLE = 4
SITES = 4096
LAT = 96
BOX = 16
PLANES = 64
N_MODE = 32


def with_ends(result, key, smallest, top_value):
    index_at = [jax.random.randint(jax.random.fold_in(key, axis), (), 0, length) for axis, length in enumerate(result.shape)]
    widest = result.shape.index(max(result.shape))
    beside = index_at[:widest] + [(index_at[widest] + 1) % result.shape[widest]] + index_at[widest + 1:]
    return result.at[tuple(index_at)].set(smallest).at[tuple(beside)].set(top_value)


def shard_levels(rng, dims, cuts, low, largest):
    def one(position, parts):
        steps = jax.random.uniform(jax.random.fold_in(jax.random.fold_in(rng, 6), position), (parts,), jnp.float32, low / len(cuts), largest / len(cuts))
        return jnp.repeat(jnp.exp(steps), dims[position] // parts).reshape((-1,) + (1,) * (len(dims) - position - 1))

    factor_of = one(*cuts[0])
    for cut in cuts[1:]:
        factor_of = factor_of * one(*cut)
    return factor_of


def scatter_about(own_key, shape, deviation, bound, pieces=(), kind=jnp.bfloat16):
    result = jax.random.normal(own_key, shape, jnp.float32) * deviation
    if len(pieces) > 0:
        result = shard_levels(own_key, shape, pieces, -0.22, 0.18) * result
    return jnp.clip(result, min=-bound, max=bound).astype(kind)


def setup_inputs(seed: int = 0) -> dict:
    seeds = jax.random.split(jax.random.key(seed), 6)
    return {
        "left_modes": scatter_about(seeds[0], (MODES, COMP, SITES), 1.0, 6.0, ((0, 32), (2, 32))),
        "right_modes": scatter_about(seeds[1], (MODES, COMP, SITES), 1.0, 6.0, ((0, 32), (2, 32))),
        "momenta": with_ends(jax.random.randint(seeds[2], (STRUCTS, 3), -3, 4), jax.random.fold_in(seeds[2], 1), -3, 3).astype(jnp.int32),
        "spin_perm": jax.vmap(lambda own: jax.random.permutation(own, 4))(jax.random.split(seeds[3], STRUCTS)).reshape((STRUCTS, 4)).astype(jnp.int32),
        "spin_phase": with_ends(jax.random.randint(seeds[4], (STRUCTS, 4), 0, 4), jax.random.fold_in(seeds[4], 1), 0, 3).astype(jnp.int32),
    }


def turned_rows(mode_rows, momenta, spin_perm, spin_phase, coords, struct_id):
    mode_count = mode_rows.shape[0]
    site_count = mode_rows.shape[2]
    real_part = mode_rows[:, :12, :].astype(jnp.float32).reshape(mode_count, 4, 3, site_count)
    imag_part = mode_rows[:, 12:, :].astype(jnp.float32).reshape(mode_count, 4, 3, site_count)
    momentum_dot = lax.optimization_barrier(jnp.sum(momenta[struct_id][:, None] * coords, axis=0))
    quarter = jnp.mod(LAT // 4 * spin_phase[struct_id][:, None] - momentum_dot[None, :], LAT)
    phase_angle = quarter.astype(jnp.float32) * (2.0 * math.pi / LAT)
    cosine = jnp.cos(phase_angle)[None, :, None, :]
    sine_val = jnp.sin(phase_angle)[None, :, None, :]
    turn_re = real_part * cosine + imag_part * sine_val
    turn_im = imag_part * cosine - real_part * sine_val
    chooser = (spin_perm[struct_id][:, None] == jnp.arange(4, dtype=jnp.int32)[None, :]).astype(jnp.float32)
    moved_re = jnp.einsum('ab,iacs->ibcs', chooser, turn_re, precision=lax.Precision.HIGHEST)
    moved_im = jnp.einsum('ab,iacs->ibcs', chooser, turn_im, precision=lax.Precision.HIGHEST)
    re_rows = jnp.concatenate([moved_re, moved_im], axis=1).reshape(mode_count, 24, site_count)
    im_rows = jnp.concatenate([-moved_im, moved_re], axis=1).reshape(mode_count, 24, site_count)
    stacked = jnp.stack([re_rows, im_rows]).astype(jnp.bfloat16)
    return stacked.reshape(2 * mode_count, 24 * site_count)

def reference(left_modes, right_modes, momenta, spin_perm, spin_phase):
    site_index = lax.iota(jnp.int32, SITES)
    coords = jnp.stack([site_index % BOX, site_index // BOX % BOX, site_index // (BOX * BOX)])
    left_blocks = left_modes.reshape(N_MODE, MODE_DEV, 24, SITES)
    right_blocks = right_modes.reshape(N_MODE, MODE_DEV, 24, SITES)

    def block_field(block_id):
        left_here = lax.dynamic_index_in_dim(left_blocks, block_id, 0, keepdims=False)
        rights = jnp.stack([lax.dynamic_index_in_dim(right_blocks, jnp.mod(block_id - shift_step, N_MODE).astype(jnp.int32), 0, keepdims=False) for shift_step in range(CYCLE)]).reshape(CYCLE * MODE_DEV, 24 * SITES)
        planes = []
        for struct_id in range(STRUCTS):
            rows_here = turned_rows(left_here, momenta, spin_perm, spin_phase, coords, struct_id)
            product = jnp.dot(rows_here, rights.T, preferred_element_type=jnp.float32)
            planes.append(product.reshape(2, MODE_DEV, CYCLE, MODE_DEV).transpose(2, 0, 1, 3))
        return jnp.stack(planes)
    fields = lax.map(block_field, jnp.arange(N_MODE, dtype=jnp.int32))
    fields = fields.transpose(1, 2, 3, 0, 4, 5).reshape(PLANES, MODES, MODE_DEV)
    return fields * (1.0 / math.sqrt(24 * SITES))
```

```python
import math

import jax
import jax.numpy as jnp
from jax import lax
from jax.experimental import pallas as pl
from jax.experimental.pallas import tpu as pltpu
from jax.sharding import PartitionSpec as P

STRUCTS = 8
LAT = 96
BOX = 16
MODES = 64
COMP = 24
PAIRS = 12
SITES = 128
PARTS = 4
PER = PAIRS // PARTS
NZ = 16
FLOAT = jnp.float32
HALF = jnp.bfloat16
MESH = pl.DeviceIdType.MESH


def kernel(
    momenta,
    perm,
    phase,
    left_hbm,
    right_hbm,
    out_ref,
    left_raw,
    right_raw,
    wide,
    angle,
    cosine,
    sine,
    left_own,
    left_far,
    right_own,
    right_far,
    rows,
    sums,
    send_one,
    take_one,
    send_two,
    take_two,
    load_sem,
    right_send,
    right_take,
    left_send,
    left_take,
    one_send,
    one_take,
    two_send,
    two_take,
):
    n_mode = lax.axis_size("mode")
    mode = lax.axis_index("mode")
    space = lax.axis_index("space")
    z = space // 2
    y = space % 2
    odd = z % 2

    def modes_on(step):
        return lax.rem(mode + step + n_mode, n_mode)

    def along(step):
        return lax.rem(z + step + NZ, NZ)

    load_left = pltpu.make_async_copy(left_hbm, left_raw, load_sem.at[0])
    load_right = pltpu.make_async_copy(right_hbm, right_raw, load_sem.at[1])
    load_right.start()
    load_left.start()

    barrier = pltpu.get_barrier_semaphore()

    def greet(to_mode, to_space):
        pl.semaphore_signal(barrier, inc=1, device_id=(to_mode, to_space), device_id_type=MESH)

    greet(modes_on(-2), space)
    greet(modes_on(1), space)
    for step in (-2, -1, 1, 2):
        greet(mode, along(step) * 2 + y)
    for turn in range(4):
        far = along(4 * turn)

        @pl.when(jnp.logical_or(y == 1, turn != 0))
        def _():
            greet(modes_on(0 - y), far * 2)

        greet(modes_on(0 - y), far * 2 + 1)

    lane = lax.broadcasted_iota(jnp.int32, (1, SITES), 1)
    first = lane % BOX
    second = (space * (SITES // BOX) + lane // BOX) % BOX
    third = space * SITES // (BOX * BOX)
    sources = []
    for struct in range(STRUCTS):
        dot = momenta[0, struct] * first + momenta[1, struct] * second + momenta[2, struct] * third
        own = []
        for spin in range(4):
            origin = jnp.int32(0)
            for other in range(1, 4):
                origin = jnp.where(perm[other, struct] == spin, other, origin)
            turn = phase[0, struct]
            for other in range(1, 4):
                turn = jnp.where(origin == other, phase[other, struct], turn)
            value = LAT // 4 * turn - dot + 2 * LAT
            quarter = value
            for times in range(1, 5):
                quarter = quarter - jnp.where(value >= times * LAT, LAT, 0)
            angle[pl.ds(struct * 4 + spin, 1), :] = quarter.astype(FLOAT) * (2.0 * math.pi / LAT)
            own.append(origin)
        sources.append(own)
    cosine[...] = jnp.cos(angle[...])
    sine[...] = jnp.sin(angle[...])

    def spread(raw):
        def step(part, carry):
            piece = raw[pl.ds(part * 8, 8)].astype(FLOAT).reshape(8 * COMP, SITES)
            wide[pl.ds(pl.multiple_of(part * 8 * COMP, 8 * COMP), 8 * COMP), :] = piece
            return carry

        lax.fori_loop(0, MODES // 8, step, 0)

    def component(index):
        return wide[pl.ds(index, MODES, stride=COMP), :]

    load_right.wait()
    spread(right_raw)
    for pair in range(PAIRS):
        real, imag = component(pair), component(PAIRS + pair)
        right_own[pair, :MODES, :SITES] = real.astype(HALF)
        right_own[pair, :MODES, SITES:] = imag.astype(HALF)
        right_own[pair, MODES:, :SITES] = imag.astype(HALF)
        right_own[pair, MODES:, SITES:] = (-real).astype(HALF)
    load_left.wait()
    spread(left_raw)
    for pair in range(PAIRS):
        left_own[pair, :, :SITES] = component(pair).astype(HALF)
        left_own[pair, :, SITES:] = component(PAIRS + pair).astype(HALF)

    @pl.when(y == 0)
    def _():
        pl.semaphore_wait(barrier, 13)

    @pl.when(y == 1)
    def _():
        pl.semaphore_wait(barrier, 14)

    left_copy = pltpu.make_async_remote_copy(
        left_own, left_far, left_send, left_take, (modes_on(-1), space), MESH
    )
    right_copies = [
        pltpu.make_async_remote_copy(
            right_own.at[pl.ds(part * PER, PER), pl.ds(0, MODES)],
            right_far.at[pl.ds(part * PER, PER), pl.ds(0, MODES)],
            right_send.at[part],
            right_take.at[part],
            (modes_on(2), space),
            MESH,
        )
        for part in range(PARTS)
    ]
    left_copy.start()
    for copy in right_copies:
        copy.start()

    def turn_rows(li):
        for struct in range(STRUCTS):
            for spin in range(4):
                origin = sources[struct][spin]
                turn_re = cosine[pl.ds(struct * 4 + spin, 1), :]
                turn_im = sine[pl.ds(struct * 4 + spin, 1), :]
                for colour in range(3):
                    block = (left_own, left_far)[li][origin * 3 + colour]
                    real = block[:, :SITES].astype(FLOAT)
                    imag = block[:, SITES:].astype(FLOAT)
                    place = rows.at[spin * 3 + colour, li * STRUCTS + struct]
                    place[:, :SITES] = (real * turn_re + imag * turn_im).astype(HALF)
                    place[:, SITES:] = (imag * turn_re - real * turn_im).astype(HALF)

    def multiply(li, rj, start, stop):
        def step(pair, carry):
            block = rows[pair, pl.ds(li * STRUCTS, STRUCTS)].reshape(STRUCTS * MODES, 2 * SITES)
            product = lax.dot_general(
                block, (right_own, right_far)[rj][pair], (((1,), (1,)), ((), ())), preferred_element_type=FLOAT
            )
            sums[rj, li] = sums[rj, li] + product.reshape(STRUCTS, MODES, 2 * MODES)
            return carry

        lax.fori_loop(start, stop, step, 0)

    def pack(li, rj):
        for struct in range(STRUCTS):
            send_one[rj, struct % 2, struct // 2, li] = sums[rj, li, struct].astype(HALF)

    def one_copies(rj):
        halfs = [lax.rem(z + NZ + step, 4) // 2 for step in (-1, 1, 2)]
        near = [
            pltpu.make_async_remote_copy(
                send_one.at[rj, halfs[side]],
                take_one.at[1 - side],
                one_send.at[rj, side],
                one_take.at[1 - side],
                (mode, along((-1, 1)[side]) * 2 + y),
                MESH,
            )
            for side in range(2)
        ]
        beyond = [
            pltpu.make_async_remote_copy(
                send_one.at[rj, halfs[2], pl.ds(2 * side, 2)],
                take_one.at[2, pl.ds(2 * side, 2)],
                one_send.at[rj, side],
                one_take.at[2 + side],
                (mode, along((2, -2)[side]) * 2 + y),
                MESH,
            )
            for side in range(2)
        ]
        return near, beyond

    def send_sums(rj):
        near, beyond = one_copies(rj)

        @pl.when(odd != rj)
        def _():
            for copy in near:
                copy.start()

        @pl.when(odd == rj)
        def _():
            for copy in beyond:
                copy.start()

    own_q = z // 4
    own_h = z % 4 // 2

    def two_copy(q, li):
        return pltpu.make_async_remote_copy(
            send_two.at[q, li],
            take_two.at[own_q, y],
            two_send.at[q, li],
            two_take.at[own_q, y],
            (modes_on(li), (q * 4 + z % 4) * 2 + li),
            MESH,
        )

    def pass_sums(rj):
        near, beyond = one_copies(rj)

        @pl.when(odd == rj)
        def _():
            for copy in near + beyond:
                copy.wait_recv()
            for q in range(4):
                for li in range(2):
                    total = sums[rj, li, q * 2 + own_h]
                    for slot in range(3):
                        total = total + take_one[slot, q, li].astype(FLOAT)
                    send_two[q, li] = total.astype(HALF)
                    if li == 0:
                        mine = jnp.logical_and(q == own_q, y == 0)

                        @pl.when(mine)
                        def _():
                            take_two[own_q, 0] = total.astype(HALF)

                        @pl.when(jnp.logical_not(mine))
                        def _():
                            two_copy(q, li).start()
                    else:
                        two_copy(q, li).start()

    sums[...] = jnp.zeros_like(sums)
    turn_rows(0)
    multiply(0, 0, 0, PAIRS)
    pack(0, 0)
    left_copy.wait_recv()
    turn_rows(1)
    multiply(1, 0, 0, PAIRS)
    pack(1, 0)
    send_sums(0)
    pass_sums(0)
    for part in range(PARTS):
        right_copies[part].wait_recv()
        for pair in range(part * PER, part * PER + PER):
            block = right_far[pair, :MODES, :]
            right_far[pair, MODES:, :SITES] = block[:, SITES:]
            right_far[pair, MODES:, SITES:] = (-block[:, :SITES].astype(FLOAT)).astype(HALF)
        for li in range(2):
            multiply(li, 1, part * PER, part * PER + PER)
    for li in range(2):
        pack(li, 1)
    send_sums(1)
    pass_sums(1)

    def two_wait(q, from_y):
        pltpu.make_async_remote_copy(
            send_two.at[0, 0],
            take_two.at[q, from_y],
            two_send.at[0, 0],
            two_take.at[q, from_y],
            (mode, space),
            MESH,
        ).wait_recv()

    total = jnp.zeros((MODES, 2 * MODES), FLOAT)
    for q in range(4):
        for from_y in range(2):
            if from_y == 0:

                @pl.when(jnp.logical_not(jnp.logical_and(q == own_q, y == 0)))
                def _():
                    two_wait(q, from_y)
            else:
                two_wait(q, from_y)
            total = total + take_two[q, from_y].astype(FLOAT)
    total = total * (1.0 / math.sqrt(COMP * SITES * NZ * 2))
    out_ref[0] = total[:, :MODES]
    out_ref[1] = total[:, MODES:]

    left_copy.wait_send()
    for copy in right_copies:
        copy.wait_send()
    for rj in range(2):
        near, beyond = one_copies(rj)

        @pl.when(odd != rj)
        def _():
            for copy in near:
                copy.wait_send()

        @pl.when(odd == rj)
        def _():
            for copy in beyond:
                copy.wait_send()

    for q in range(4):
        for li in range(2):

            @pl.when(jnp.logical_not(jnp.logical_and(jnp.logical_and(q == own_q, y == 0), li == 0)))
            def _():
                two_copy(q, li).wait_send()


def solution(mesh):
    def local(left_modes, right_modes, momenta, spin_perm, spin_phase):
        small = pl.BlockSpec(memory_space=pltpu.SMEM)
        large = pl.BlockSpec(memory_space=pl.ANY)
        dma = pltpu.SemaphoreType.DMA
        return pl.pallas_call(
            kernel,
            out_shape=jax.ShapeDtypeStruct((2, MODES, MODES), FLOAT),
            in_specs=[small, small, small, large, large],
            out_specs=pl.BlockSpec(memory_space=pltpu.VMEM),
            scratch_shapes=[
                pltpu.VMEM((MODES, COMP, SITES), HALF),
                pltpu.VMEM((MODES, COMP, SITES), HALF),
                pltpu.VMEM((MODES * COMP, SITES), FLOAT),
                pltpu.VMEM((STRUCTS * 4, SITES), FLOAT),
                pltpu.VMEM((STRUCTS * 4, SITES), FLOAT),
                pltpu.VMEM((STRUCTS * 4, SITES), FLOAT),
                pltpu.VMEM((PAIRS, MODES, 2 * SITES), HALF),
                pltpu.VMEM((PAIRS, MODES, 2 * SITES), HALF),
                pltpu.VMEM((PAIRS, 2 * MODES, 2 * SITES), HALF),
                pltpu.VMEM((PAIRS, 2 * MODES, 2 * SITES), HALF),
                pltpu.VMEM((PAIRS, 2 * STRUCTS, MODES, 2 * SITES), HALF),
                pltpu.VMEM((2, 2, STRUCTS, MODES, 2 * MODES), FLOAT),
                pltpu.VMEM((2, 2, 4, 2, MODES, 2 * MODES), HALF),
                pltpu.VMEM((3, 4, 2, MODES, 2 * MODES), HALF),
                pltpu.VMEM((4, 2, MODES, 2 * MODES), HALF),
                pltpu.VMEM((4, 2, MODES, 2 * MODES), HALF),
                dma((2,)),
                dma((PARTS,)),
                dma((PARTS,)),
                dma,
                dma,
                dma((2, 2)),
                dma((4,)),
                dma((4, 2)),
                dma((4, 2)),
            ],
            compiler_params=pltpu.CompilerParams(
                collective_id=0, has_side_effects=True, vmem_limit_bytes=40 * 2**20
            ),
            cost_estimate=pl.CostEstimate(
                flops=2 * 1024 * 256 * 3072, bytes_accessed=2**20, transcendentals=8192
            ),
        )(momenta.T, spin_perm.T, spin_phase.T, left_modes, right_modes)

    placed = (P("mode", None, "space"), P("mode", None, "space"), P(), P(), P())
    return jax.shard_map(
        local, mesh=mesh, in_specs=placed, out_specs=P("space", "mode", None), check_vma=False
    )
```

```python
import math

import jax
import jax.numpy as jnp
from jax import lax
from jax.experimental import pallas as pl
from jax.experimental.pallas import tpu as pltpu
from jax.sharding import PartitionSpec as P

STRUCTS = 8
LAT = 96
BOX = 16
MODES = 64
COMP = 24
PAIRS = 12
SITES = 128
PARTS = 6
PER = PAIRS // PARTS
RELAYED = (3, 4, 5)
NZ = 16
ROW = 8
SLOTS = 6
FLOAT = jnp.float32
HALF = jnp.bfloat16
MESH = pl.DeviceIdType.MESH


def kernel(
    momenta_hbm,
    perm_hbm,
    phase_hbm,
    left_hbm,
    right_hbm,
    out_ref,
    momenta,
    perm,
    phase,
    left_raw,
    right_raw,
    wide,
    angle,
    cosine,
    sine,
    left_own,
    left_far,
    right_own,
    right_far,
    relay,
    rows,
    sums,
    send_one,
    take_one,
    send_two,
    take_two,
    load_sem,
    right_send,
    right_take,
    relay_take,
    relay_send,
    left_send,
    left_take,
    one_send,
    one_take,
    two_send,
    two_take,
):
    n_mode = lax.axis_size("mode")
    mode = lax.axis_index("mode")
    space = lax.axis_index("space")
    z = space // 2
    y = space % 2
    odd = z % 2
    in_row = lax.rem(mode, ROW)
    first_chip = in_row < 2
    last_chip = in_row >= ROW - 2

    def modes_on(step):
        return lax.rem(mode + step + n_mode, n_mode)

    def along(step):
        return lax.rem(z + step + NZ, NZ)

    loads = [
        pltpu.make_async_copy(source, target, load_sem.at[index])
        for index, (source, target) in enumerate(
            (
                (right_hbm, right_raw),
                (left_hbm, left_raw),
                (momenta_hbm, momenta),
                (perm_hbm, perm),
                (phase_hbm, phase),
            )
        )
    ]
    for load in loads:
        load.start()

    barrier = pltpu.get_barrier_semaphore()

    def greet(to_mode, to_space):
        pl.semaphore_signal(barrier, inc=1, device_id=(to_mode, to_space), device_id_type=MESH)

    greet(modes_on(-2), space)
    greet(modes_on(1), space)

    @pl.when(first_chip)
    def _():
        greet(mode + ROW - 2, space)
        greet(modes_on(-ROW), space)

    for step in (-2, -1, 1, 2, 3):
        greet(mode, along(step) * 2 + y)
    for step in (0, 5, -5):
        if step == 0:

            @pl.when(y == 1)
            def _():
                greet(modes_on(0 - y), z * 2)
        else:
            greet(modes_on(0 - y), along(step) * 2)
        greet(modes_on(0 - y), along(step) * 2 + 1)

    def spread(raw):
        def step(part, carry):
            piece = raw[pl.ds(part * 8, 8)].astype(FLOAT).reshape(8 * COMP, SITES)
            wide[pl.ds(pl.multiple_of(part * 8 * COMP, 8 * COMP), 8 * COMP), :] = piece
            return carry

        lax.fori_loop(0, MODES // 8, step, 0)

    def component(index):
        return wide[pl.ds(index, MODES, stride=COMP), :]

    loads[0].wait()
    spread(right_raw)
    for pair in range(PAIRS):
        real, imag = component(pair), component(PAIRS + pair)
        right_own[pair, :MODES, :SITES] = real.astype(HALF)
        right_own[pair, :MODES, SITES:] = imag.astype(HALF)
        right_own[pair, MODES:, :SITES] = imag.astype(HALF)
        right_own[pair, MODES:, SITES:] = (-real).astype(HALF)
    loads[1].wait()
    spread(left_raw)
    for pair in range(PAIRS):
        left_own[pair, :, :SITES] = component(pair).astype(HALF)
        left_own[pair, :, SITES:] = component(PAIRS + pair).astype(HALF)

    edge = jnp.logical_or(first_chip, last_chip)
    pl.semaphore_wait(barrier, 12 + y + edge.astype(jnp.int32))

    def part_of(ref, part):
        return ref.at[pl.ds(part * PER, PER), pl.ds(0, MODES)]

    def right_copy(part):
        return pltpu.make_async_remote_copy(
            part_of(right_own, part),
            part_of(right_far, part),
            right_send.at[part],
            right_take.at[part],
            (modes_on(2), space),
            MESH,
        )

    def aside_copy(turn):
        return pltpu.make_async_remote_copy(
            part_of(right_own, RELAYED[turn]),
            relay.at[turn],
            right_send.at[RELAYED[turn]],
            relay_take.at[turn],
            (modes_on(2 - ROW), space),
            MESH,
        )

    def relay_copy(turn):
        return pltpu.make_async_remote_copy(
            relay.at[turn],
            part_of(right_far, RELAYED[turn]),
            relay_send.at[turn],
            right_take.at[RELAYED[turn]],
            (modes_on(ROW), space),
            MESH,
        )

    left_copy = pltpu.make_async_remote_copy(
        left_own, left_far, left_send, left_take, (modes_on(-1), space), MESH
    )

    @pl.when(last_chip)
    def _():
        for turn in range(len(RELAYED)):
            aside_copy(turn).start()

    for part in range(PARTS):
        if part not in RELAYED:
            right_copy(part).start()
    left_copy.start()

    @pl.when(jnp.logical_not(last_chip))
    def _():
        for part in RELAYED:
            right_copy(part).start()

    for load in loads[2:]:
        load.wait()

    lane = lax.broadcasted_iota(jnp.int32, (1, SITES), 1)
    first = lane % BOX
    second = (space * (SITES // BOX) + lane // BOX) % BOX
    third = space * SITES // (BOX * BOX)
    sources = []
    for struct in range(STRUCTS):
        dot = momenta[0, struct] * first + momenta[1, struct] * second + momenta[2, struct] * third
        own = []
        for spin in range(4):
            origin = jnp.int32(0)
            for other in range(1, 4):
                origin = jnp.where(perm[other, struct] == spin, other, origin)
            turn = phase[0, struct]
            for other in range(1, 4):
                turn = jnp.where(origin == other, phase[other, struct], turn)
            value = LAT // 4 * turn - dot + 2 * LAT
            quarter = value
            for times in range(1, 5):
                quarter = quarter - jnp.where(value >= times * LAT, LAT, 0)
            angle[pl.ds(struct * 4 + spin, 1), :] = quarter.astype(FLOAT) * (2.0 * math.pi / LAT)
            own.append(origin)
        sources.append(own)
    cosine[...] = jnp.cos(angle[...])
    sine[...] = jnp.sin(angle[...])

    def turn_rows(li):
        for struct in range(STRUCTS):
            for spin in range(4):
                origin = sources[struct][spin]
                turn_re = cosine[pl.ds(struct * 4 + spin, 1), :]
                turn_im = sine[pl.ds(struct * 4 + spin, 1), :]
                for colour in range(3):
                    block = (left_own, left_far)[li][origin * 3 + colour]
                    real = block[:, :SITES].astype(FLOAT)
                    imag = block[:, SITES:].astype(FLOAT)
                    place = rows.at[spin * 3 + colour, li, struct]
                    place[:, :SITES] = (real * turn_re + imag * turn_im).astype(HALF)
                    place[:, SITES:] = (imag * turn_re - real * turn_im).astype(HALF)

    def product(blocks, right, pairs):
        total = None
        for pair in pairs:
            left = jnp.concatenate(
                [rows[pair, li, a:b].reshape((b - a) * MODES, 2 * SITES) for li, a, b in blocks], axis=0
            )
            term = lax.dot_general(
                left, right[pair], (((1,), (1,)), ((), ())), preferred_element_type=FLOAT
            )
            total = term if total is None else total + term
        return total.reshape(-1, MODES, 2 * MODES)

    def near_sums(li):
        total = product([(li, 0, STRUCTS)], right_own, range(PAIRS))
        sums[0, li] = total
        for struct in range(STRUCTS):
            send_one[0, struct, li] = total[struct].astype(HALF)

    def far_arrive(parts):
        for part in parts:
            right_copy(part).wait_recv()
            for pair in range(part * PER, part * PER + PER):
                block = right_far[pair, :MODES, :]
                right_far[pair, MODES:, :SITES] = block[:, SITES:]
                right_far[pair, MODES:, SITES:] = (-block[:, :SITES].astype(FLOAT)).astype(HALF)

    def far_sums(li, pairs, fresh):
        total = product([(li, 0, STRUCTS)], right_far, pairs)
        sums[1, li] = total if fresh else sums[1, li] + total

    def one_place(rj, struct):
        to = 2 * struct + rj
        gap = lax.rem(z - to + NZ, NZ)
        plus = jnp.logical_and(gap >= 3, gap <= 8)
        minus = jnp.logical_and(gap >= 9, gap <= 13)
        role = jnp.where(plus, 1, jnp.where(minus, 2, 0))
        adder = lax.rem(to + jnp.where(plus, 5, jnp.where(minus, NZ - 5, 0)), NZ)
        slot = lax.rem(z - adder + NZ + 2, NZ)
        return adder, role, slot

    def one_copy(rj, struct):
        adder, role, slot = one_place(rj, struct)
        return adder != z, pltpu.make_async_remote_copy(
            send_one.at[rj, struct],
            take_one.at[role, slot],
            one_send.at[rj, struct],
            one_take.at[role, slot],
            (mode, adder * 2 + y),
            MESH,
        )

    def send_sums(rj, struct):
        away, copy = one_copy(rj, struct)

        @pl.when(away)
        def _():
            copy.start()

    def owner_z(role):
        return along((0, -5, 5)[role])

    def two_copy(role, li):
        return pltpu.make_async_remote_copy(
            send_two.at[role, li],
            take_two.at[role, y],
            two_send.at[role, li],
            two_take.at[role, y],
            (modes_on(li), owner_z(role) * 2 + li),
            MESH,
        )

    def add_and_pass(role):
        slots = (0, 1, 3, 4, 5) if role == 1 else (0, 1, 3, 4)
        for slot in slots:
            pltpu.make_async_remote_copy(
                send_one.at[0, 0],
                take_one.at[role, slot],
                one_send.at[0, 0],
                one_take.at[role, slot],
                (mode, space),
                MESH,
            ).wait_recv()
        to = owner_z(role)
        for li in range(2):
            total = sums[to % 2, li, to // 2]
            for slot in slots:
                total = total + take_one[role, slot, li].astype(FLOAT)
            send_two[role, li] = total.astype(HALF)
            if role == 0 and li == 0:

                @pl.when(y == 0)
                def _():
                    take_two[0, 0] = total.astype(HALF)

                @pl.when(y == 1)
                def _():
                    two_copy(role, li).start()
            else:
                two_copy(role, li).start()

    def pass_sums(rj):
        @pl.when(odd == rj)
        def _():
            add_and_pass(0)

        @pl.when(odd != rj)
        def _():
            add_and_pass(1)
            add_and_pass(2)

    def hand_on(turn):
        @pl.when(first_chip)
        def _():
            aside_copy(turn).wait_recv()
            relay_copy(turn).start()

    turn_rows(0)
    hand_on(0)
    near_sums(0)
    hand_on(1)
    left_copy.wait_recv()
    turn_rows(1)
    hand_on(2)
    near_sums(1)
    for struct in range(STRUCTS):
        send_sums(0, struct)
    far_arrive((0, 1, 2))
    for li in range(2):
        far_sums(li, range(0, 3 * PER), True)
    pass_sums(0)
    far_arrive((3, 4))
    for li in range(2):
        far_sums(li, range(3 * PER, 5 * PER), False)
    far_arrive((5,))
    for q in range(STRUCTS // 2):
        last = product([(0, 2 * q, 2 * q + 2), (1, 2 * q, 2 * q + 2)], right_far, range(5 * PER, PAIRS))
        for struct in (2 * q, 2 * q + 1):
            for li in range(2):
                total = sums[1, li, struct] + last[2 * li + struct % 2]
                sums[1, li, struct] = total
                send_one[1, struct, li] = total.astype(HALF)
            send_sums(1, struct)
    pass_sums(1)

    total = jnp.zeros((MODES, 2 * MODES), FLOAT)
    for role in range(3):
        for from_y in range(2):
            arrived = pltpu.make_async_remote_copy(
                send_two.at[0, 0],
                take_two.at[role, from_y],
                two_send.at[0, 0],
                two_take.at[role, from_y],
                (mode, space),
                MESH,
            )
            if role == 0 and from_y == 0:

                @pl.when(y == 1)
                def _():
                    arrived.wait_recv()
            else:
                arrived.wait_recv()
            total = total + take_two[role, from_y].astype(FLOAT)
    total = total * (1.0 / math.sqrt(COMP * SITES * NZ * 2))
    out_ref[0] = total[:, :MODES]
    out_ref[1] = total[:, MODES:]

    left_copy.wait_send()
    for part in range(PARTS):
        right_copy(part).wait_send()

    @pl.when(first_chip)
    def _():
        for turn in range(len(RELAYED)):
            relay_copy(turn).wait_send()

    for rj in range(2):
        for struct in range(STRUCTS):
            away, copy = one_copy(rj, struct)

            @pl.when(away)
            def _():
                copy.wait_send()

    for role in range(3):
        for li in range(2):
            if role == 0 and li == 0:

                @pl.when(y == 1)
                def _():
                    two_copy(role, li).wait_send()
            else:
                two_copy(role, li).wait_send()


def solution(mesh):
    def local(left_modes, right_modes, momenta, spin_perm, spin_phase):
        large = pl.BlockSpec(memory_space=pl.ANY)
        dma = pltpu.SemaphoreType.DMA
        return pl.pallas_call(
            kernel,
            out_shape=jax.ShapeDtypeStruct((2, MODES, MODES), FLOAT),
            in_specs=[large] * 5,
            out_specs=pl.BlockSpec(memory_space=pltpu.VMEM),
            scratch_shapes=[
                pltpu.SMEM((3, STRUCTS), jnp.int32),
                pltpu.SMEM((4, STRUCTS), jnp.int32),
                pltpu.SMEM((4, STRUCTS), jnp.int32),
                pltpu.VMEM((MODES, COMP, SITES), HALF),
                pltpu.VMEM((MODES, COMP, SITES), HALF),
                pltpu.VMEM((MODES * COMP, SITES), FLOAT),
                pltpu.VMEM((STRUCTS * 4, SITES), FLOAT),
                pltpu.VMEM((STRUCTS * 4, SITES), FLOAT),
                pltpu.VMEM((STRUCTS * 4, SITES), FLOAT),
                pltpu.VMEM((PAIRS, MODES, 2 * SITES), HALF),
                pltpu.VMEM((PAIRS, MODES, 2 * SITES), HALF),
                pltpu.VMEM((PAIRS, 2 * MODES, 2 * SITES), HALF),
                pltpu.VMEM((PAIRS, 2 * MODES, 2 * SITES), HALF),
                pltpu.VMEM((len(RELAYED), PER, MODES, 2 * SITES), HALF),
                pltpu.VMEM((PAIRS, 2, STRUCTS, MODES, 2 * SITES), HALF),
                pltpu.VMEM((2, 2, STRUCTS, MODES, 2 * MODES), FLOAT),
                pltpu.VMEM((2, STRUCTS, 2, MODES, 2 * MODES), HALF),
                pltpu.VMEM((3, SLOTS, 2, MODES, 2 * MODES), HALF),
                pltpu.VMEM((3, 2, MODES, 2 * MODES), HALF),
                pltpu.VMEM((3, 2, MODES, 2 * MODES), HALF),
                dma((5,)),
                dma((PARTS,)),
                dma((PARTS,)),
                dma((len(RELAYED),)),
                dma((len(RELAYED),)),
                dma,
                dma,
                dma((2, STRUCTS)),
                dma((3, SLOTS)),
                dma((3, 2)),
                dma((3, 2)),
            ],
            compiler_params=pltpu.CompilerParams(
                collective_id=0, has_side_effects=True, vmem_limit_bytes=60 * 2**20
            ),
            cost_estimate=pl.CostEstimate(
                flops=2 * 1024 * 256 * 3072, bytes_accessed=2**20, transcendentals=8192
            ),
        )(momenta.T, spin_perm.T, spin_phase.T, left_modes, right_modes)

    placed = (P("mode", None, "space"), P("mode", None, "space"), P(), P(), P())
    return jax.shard_map(
        local, mesh=mesh, in_specs=placed, out_specs=P("space", "mode", None), check_vma=False
    )
```

```python
import math

import jax
import jax.numpy as jnp
from jax import lax
from jax.experimental import pallas as pl
from jax.experimental.pallas import tpu as pltpu
from jax.sharding import PartitionSpec as P

STRUCTS = 8
LAT = 96
BOX = 16
MODES = 64
COMP = 24
PAIRS = 12
SITES = 128
PARTS = 12
PER = PAIRS // PARTS
RELAYED = (8, 9, 10, 11)
LEFT_CUTS = ((0, 8), (8, 2), (10, 2))
NZ = 16
ROW = 8
SLOTS = 7
FLOAT = jnp.float32
HALF = jnp.bfloat16
MESH = pl.DeviceIdType.MESH


def kernel(
    momenta_hbm,
    perm_hbm,
    phase_hbm,
    left_hbm,
    right_hbm,
    out_ref,
    momenta,
    perm,
    phase,
    left_raw,
    right_raw,
    wide,
    angle,
    cosine,
    sine,
    left_own,
    left_far,
    right_own,
    right_far,
    relay,
    left_relay,
    rows,
    sums,
    send_one,
    take_one,
    send_two,
    take_two,
    load_sem,
    right_send,
    right_take,
    relay_take,
    relay_send,
    left_send,
    left_take,
    aside_take,
    aside_send,
    one_send,
    one_take,
    two_send,
    two_take,
):
    n_mode = lax.axis_size("mode")
    mode = lax.axis_index("mode")
    space = lax.axis_index("space")
    z = space // 2
    y = space % 2
    odd = z % 2
    in_row = lax.rem(mode, ROW)
    first_chip = in_row < 2
    last_chip = in_row >= ROW - 2

    def modes_on(step):
        return lax.rem(mode + step + n_mode, n_mode)

    def along(step):
        return lax.rem(z + step + NZ, NZ)

    loads = [
        pltpu.make_async_copy(source, target, load_sem.at[index])
        for index, (source, target) in enumerate(
            (
                (right_hbm, right_raw),
                (left_hbm, left_raw),
                (momenta_hbm, momenta),
                (perm_hbm, perm),
                (phase_hbm, phase),
            )
        )
    ]
    barrier = pltpu.get_barrier_semaphore()

    def greet(to_mode, to_space):
        pl.semaphore_signal(barrier, inc=1, device_id=(to_mode, to_space), device_id_type=MESH)

    for step in (5, -5, 0):
        if step == 0:

            @pl.when(y == 1)
            def _():
                greet(modes_on(0 - y), z * 2)
        else:
            greet(modes_on(0 - y), along(step) * 2)
        greet(modes_on(0 - y), along(step) * 2 + 1)

    for load in loads:
        load.start()

    for step in (3, -3, -2, 2, -1, 1):
        greet(mode, along(step) * 2 + y)

    greet(modes_on(-2), space)
    greet(modes_on(1), space)

    @pl.when(first_chip)
    def _():
        greet(mode + ROW - 2, space)
        greet(modes_on(-ROW), space)

    @pl.when(in_row == ROW - 1)
    def _():
        greet(mode - ROW + 1, space)
        greet(modes_on(ROW), space)

    def spread(raw):
        def step(part, carry):
            piece = raw[pl.ds(part * 8, 8)].astype(FLOAT).reshape(8 * COMP, SITES)
            wide[pl.ds(pl.multiple_of(part * 8 * COMP, 8 * COMP), 8 * COMP), :] = piece
            return carry

        lax.fori_loop(0, MODES // 8, step, 0)

    def component(index):
        return wide[pl.ds(index, MODES, stride=COMP), :]

    loads[0].wait()
    spread(right_raw)
    for pair in range(PAIRS):
        real, imag = component(pair), component(PAIRS + pair)
        right_own[pair, :MODES, :SITES] = real.astype(HALF)
        right_own[pair, :MODES, SITES:] = imag.astype(HALF)
        right_own[pair, MODES:, :SITES] = imag.astype(HALF)
        right_own[pair, MODES:, SITES:] = (-real).astype(HALF)
    loads[1].wait()
    spread(left_raw)
    for pair in range(PAIRS):
        left_own[pair, :, :SITES] = component(pair).astype(HALF)
        left_own[pair, :, SITES:] = component(PAIRS + pair).astype(HALF)

    edge = jnp.logical_or(first_chip, last_chip)
    ends = jnp.logical_or(in_row == 0, in_row == ROW - 1)
    pl.semaphore_wait(barrier, 13 + y + edge.astype(jnp.int32) + ends.astype(jnp.int32))

    def part_of(ref, part):
        return ref.at[pl.ds(part * PER, PER), pl.ds(0, MODES)]

    def right_copy(part):
        return pltpu.make_async_remote_copy(
            part_of(right_own, part),
            part_of(right_far, part),
            right_send.at[part],
            right_take.at[part],
            (modes_on(2), space),
            MESH,
        )

    def aside_copy(turn):
        return pltpu.make_async_remote_copy(
            part_of(right_own, RELAYED[turn]),
            relay.at[turn],
            right_send.at[RELAYED[turn]],
            relay_take.at[turn],
            (modes_on(2 - ROW), space),
            MESH,
        )

    def relay_copy(turn):
        return pltpu.make_async_remote_copy(
            relay.at[turn],
            part_of(right_far, RELAYED[turn]),
            relay_send.at[turn],
            right_take.at[RELAYED[turn]],
            (modes_on(ROW), space),
            MESH,
        )

    def left_part(ref, cut):
        start, size = LEFT_CUTS[cut]
        return ref.at[pl.ds(start, size)]

    def left_copy(cut):
        return pltpu.make_async_remote_copy(
            left_part(left_own, cut),
            left_part(left_far, cut),
            left_send.at[cut],
            left_take.at[cut],
            (modes_on(-1), space),
            MESH,
        )

    def left_aside(cut):
        return pltpu.make_async_remote_copy(
            left_part(left_own, cut),
            left_relay.at[cut - 1],
            left_send.at[cut],
            aside_take.at[cut - 1],
            (modes_on(ROW - 1), space),
            MESH,
        )

    def left_on(cut):
        return pltpu.make_async_remote_copy(
            left_relay.at[cut - 1],
            left_part(left_far, cut),
            aside_send.at[cut - 1],
            left_take.at[cut],
            (modes_on(-ROW), space),
            MESH,
        )

    def start_aside(turn):
        @pl.when(last_chip)
        def _():
            aside_copy(turn).start()

    start_aside(0)

    @pl.when(in_row == 0)
    def _():
        left_aside(1).start()
        left_aside(2).start()

    left_copy(0).start()

    @pl.when(in_row != 0)
    def _():
        left_copy(1).start()
        left_copy(2).start()

    for part in range(PARTS):
        if part not in RELAYED:
            right_copy(part).start()

    @pl.when(jnp.logical_not(last_chip))
    def _():
        for part in RELAYED:
            right_copy(part).start()

    start_aside(1)
    for load in loads[2:]:
        load.wait()

    lane = lax.broadcasted_iota(jnp.int32, (1, SITES), 1)
    first = lane % BOX
    second = (space * (SITES // BOX) + lane // BOX) % BOX
    third = space * SITES // (BOX * BOX)
    sources = []
    for struct in range(STRUCTS):
        dot = momenta[0, struct] * first + momenta[1, struct] * second + momenta[2, struct] * third
        own = []
        for spin in range(4):
            origin = jnp.int32(0)
            for other in range(1, 4):
                origin = jnp.where(perm[other, struct] == spin, other, origin)
            turn = phase[0, struct]
            for other in range(1, 4):
                turn = jnp.where(origin == other, phase[other, struct], turn)
            value = LAT // 4 * turn - dot + 2 * LAT
            quarter = value
            for times in range(1, 5):
                quarter = quarter - jnp.where(value >= times * LAT, LAT, 0)
            angle[pl.ds(struct * 4 + spin, 1), :] = quarter.astype(FLOAT) * (2.0 * math.pi / LAT)
            own.append(origin)
        sources.append(own)
        if struct % 4 == 3:
            start_aside(2 + struct // 4)
    cosine[...] = jnp.cos(angle[...])
    sine[...] = jnp.sin(angle[...])

    def turn_rows(li, structs):
        for struct in structs:
            for spin in range(4):
                origin = sources[struct][spin]
                turn_re = cosine[pl.ds(struct * 4 + spin, 1), :]
                turn_im = sine[pl.ds(struct * 4 + spin, 1), :]
                for colour in range(3):
                    block = (left_own, left_far)[li][origin * 3 + colour]
                    real = block[:, :SITES].astype(FLOAT)
                    imag = block[:, SITES:].astype(FLOAT)
                    place = rows.at[spin * 3 + colour, li, struct]
                    place[:, :SITES] = (real * turn_re + imag * turn_im).astype(HALF)
                    place[:, SITES:] = (imag * turn_re - real * turn_im).astype(HALF)

    def product(blocks, right, pairs):
        total = None
        for pair in pairs:
            left = jnp.concatenate(
                [rows[pair, li, a:b].reshape((b - a) * MODES, 2 * SITES) for li, a, b in blocks], axis=0
            )
            term = lax.dot_general(
                left, right[pair], (((1,), (1,)), ((), ())), preferred_element_type=FLOAT
            )
            total = term if total is None else total + term
        return total.reshape(-1, MODES, 2 * MODES)

    def near_sums(li):
        total = product([(li, 0, STRUCTS)], right_own, range(PAIRS))
        sums[0, li] = total
        for struct in range(STRUCTS):
            send_one[0, struct, li] = total[struct].astype(HALF)

    def far_arrive(parts):
        for part in parts:
            right_copy(part).wait_recv()
            for pair in range(part * PER, part * PER + PER):
                block = right_far[pair, :MODES, :]
                right_far[pair, MODES:, :SITES] = block[:, SITES:]
                right_far[pair, MODES:, SITES:] = (-block[:, :SITES].astype(FLOAT)).astype(HALF)

    def far_sums(li, pairs, fresh):
        total = product([(li, 0, STRUCTS)], right_far, pairs)
        sums[1, li] = total if fresh else sums[1, li] + total

    def one_place(rj, struct):
        to = 2 * struct + rj
        gap = lax.rem(z - to + NZ, NZ)
        middle = 8 if to < NZ // 2 else 7
        plus = jnp.logical_and(gap >= 3, gap <= middle)
        minus = jnp.logical_and(gap > middle, gap <= 13)
        role = jnp.where(plus, 1, jnp.where(minus, 2, 0))
        adder = lax.rem(to + jnp.where(plus, 5, jnp.where(minus, NZ - 5, 0)), NZ)
        slot = lax.rem(z - adder + NZ + 3, NZ)
        return adder, role, slot

    def one_copy(rj, struct):
        adder, role, slot = one_place(rj, struct)
        return adder != z, pltpu.make_async_remote_copy(
            send_one.at[rj, struct],
            take_one.at[role, slot],
            one_send.at[rj, struct],
            one_take.at[role, slot],
            (mode, adder * 2 + y),
            MESH,
        )

    def send_sums(rj, struct):
        away, copy = one_copy(rj, struct)

        @pl.when(away)
        def _():
            copy.start()

    def owner_z(role):
        return along((0, -5, 5)[role])

    def two_copy(role, li):
        return pltpu.make_async_remote_copy(
            send_two.at[role, li],
            take_two.at[role, y],
            two_send.at[role, li],
            two_take.at[role, y],
            (modes_on(li), owner_z(role) * 2 + li),
            MESH,
        )

    def add_and_pass(role):
        slots = (1, 2, 4, 5)
        if role == 0:
            add_slots(role, slots)
            return
        low = owner_z(role) < NZ // 2
        more = low if role == 1 else jnp.logical_not(low)

        @pl.when(more)
        def _():
            add_slots(role, slots + ((6,) if role == 1 else (0,)))

        @pl.when(jnp.logical_not(more))
        def _():
            add_slots(role, slots)

    def add_slots(role, slots):
        for slot in slots:
            pltpu.make_async_remote_copy(
                send_one.at[0, 0],
                take_one.at[role, slot],
                one_send.at[0, 0],
                one_take.at[role, slot],
                (mode, space),
                MESH,
            ).wait_recv()
        to = owner_z(role)
        for li in range(2):
            total = sums[to % 2, li, to // 2]
            for slot in slots:
                total = total + take_one[role, slot, li].astype(FLOAT)
            send_two[role, li] = total.astype(HALF)
            if role == 0 and li == 0:

                @pl.when(y == 0)
                def _():
                    take_two[0, 0] = total.astype(HALF)

                @pl.when(y == 1)
                def _():
                    two_copy(role, li).start()
            else:
                two_copy(role, li).start()

    def pass_sums(rj):
        @pl.when(odd == rj)
        def _():
            add_and_pass(0)

        @pl.when(odd != rj)
        def _():
            back = jnp.logical_and(z >= 5, z < 11)

            @pl.when(back)
            def _():
                add_and_pass(1)

            add_and_pass(2)

            @pl.when(jnp.logical_not(back))
            def _():
                add_and_pass(1)

    def hand_on(turn):
        @pl.when(first_chip)
        def _():
            aside_copy(turn).wait_recv()
            relay_copy(turn).start()

    def left_hand_on(cut):
        @pl.when(in_row == ROW - 1)
        def _():
            left_aside(cut).wait_recv()
            left_on(cut).start()

    turn_rows(0, range(0, 4))
    if len(RELAYED) > 4:
        start_aside(4)
    turn_rows(0, range(4, STRUCTS))
    if len(RELAYED) > 5:
        start_aside(5)
    hand_on(0)
    hand_on(1)
    left_hand_on(1)
    near_sums(0)
    left_hand_on(2)
    for turn in range(2, len(RELAYED)):
        hand_on(turn)
    for cut in range(len(LEFT_CUTS)):
        left_copy(cut).wait_recv()
    turn_rows(1, range(STRUCTS))
    near_sums(1)
    for struct in range(STRUCTS):
        send_sums(0, struct)
    far_arrive(range(0, 6))
    for li in range(2):
        far_sums(li, range(0, 6), True)
    pass_sums(0)
    far_arrive(range(6, 10))
    for li in range(2):
        far_sums(li, range(6, 10), False)
    far_arrive(range(10, PARTS))
    for q in range(STRUCTS // 2):
        last = product([(0, 2 * q, 2 * q + 2), (1, 2 * q, 2 * q + 2)], right_far, range(10, PAIRS))
        for struct in (2 * q, 2 * q + 1):
            for li in range(2):
                total = sums[1, li, struct] + last[2 * li + struct % 2]
                sums[1, li, struct] = total
                send_one[1, struct, li] = total.astype(HALF)
            send_sums(1, struct)
    pass_sums(1)

    total = jnp.zeros((MODES, 2 * MODES), FLOAT)
    for role in range(3):
        for from_y in range(2):
            arrived = pltpu.make_async_remote_copy(
                send_two.at[0, 0],
                take_two.at[role, from_y],
                two_send.at[0, 0],
                two_take.at[role, from_y],
                (mode, space),
                MESH,
            )
            if role == 0 and from_y == 0:

                @pl.when(y == 1)
                def _():
                    arrived.wait_recv()
            else:
                arrived.wait_recv()
            total = total + take_two[role, from_y].astype(FLOAT)
    total = total * (1.0 / math.sqrt(COMP * SITES * NZ * 2))
    out_ref[0] = total[:, :MODES]
    out_ref[1] = total[:, MODES:]

    for cut in range(len(LEFT_CUTS)):
        left_copy(cut).wait_send()
    for part in range(PARTS):
        right_copy(part).wait_send()

    @pl.when(first_chip)
    def _():
        for turn in range(len(RELAYED)):
            relay_copy(turn).wait_send()

    @pl.when(in_row == ROW - 1)
    def _():
        for cut in (1, 2):
            left_on(cut).wait_send()

    for rj in range(2):
        for struct in range(STRUCTS):
            away, copy = one_copy(rj, struct)

            @pl.when(away)
            def _():
                copy.wait_send()

    for role in range(3):
        for li in range(2):
            if role == 0 and li == 0:

                @pl.when(y == 1)
                def _():
                    two_copy(role, li).wait_send()
            else:
                two_copy(role, li).wait_send()


def solution(mesh):
    def local(left_modes, right_modes, momenta, spin_perm, spin_phase):
        large = pl.BlockSpec(memory_space=pl.ANY)
        dma = pltpu.SemaphoreType.DMA
        return pl.pallas_call(
            kernel,
            out_shape=jax.ShapeDtypeStruct((2, MODES, MODES), FLOAT),
            in_specs=[large] * 5,
            out_specs=pl.BlockSpec(memory_space=pltpu.VMEM),
            scratch_shapes=[
                pltpu.SMEM((3, STRUCTS), jnp.int32),
                pltpu.SMEM((4, STRUCTS), jnp.int32),
                pltpu.SMEM((4, STRUCTS), jnp.int32),
                pltpu.VMEM((MODES, COMP, SITES), HALF),
                pltpu.VMEM((MODES, COMP, SITES), HALF),
                pltpu.VMEM((MODES * COMP, SITES), FLOAT),
                pltpu.VMEM((STRUCTS * 4, SITES), FLOAT),
                pltpu.VMEM((STRUCTS * 4, SITES), FLOAT),
                pltpu.VMEM((STRUCTS * 4, SITES), FLOAT),
                pltpu.VMEM((PAIRS, MODES, 2 * SITES), HALF),
                pltpu.VMEM((PAIRS, MODES, 2 * SITES), HALF),
                pltpu.VMEM((PAIRS, 2 * MODES, 2 * SITES), HALF),
                pltpu.VMEM((PAIRS, 2 * MODES, 2 * SITES), HALF),
                pltpu.VMEM((len(RELAYED), PER, MODES, 2 * SITES), HALF),
                pltpu.VMEM((2, 2, MODES, 2 * SITES), HALF),
                pltpu.VMEM((PAIRS, 2, STRUCTS, MODES, 2 * SITES), HALF),
                pltpu.VMEM((2, 2, STRUCTS, MODES, 2 * MODES), FLOAT),
                pltpu.VMEM((2, STRUCTS, 2, MODES, 2 * MODES), HALF),
                pltpu.VMEM((3, SLOTS, 2, MODES, 2 * MODES), HALF),
                pltpu.VMEM((3, 2, MODES, 2 * MODES), HALF),
                pltpu.VMEM((3, 2, MODES, 2 * MODES), HALF),
                dma((5,)),
                dma((PARTS,)),
                dma((PARTS,)),
                dma((len(RELAYED),)),
                dma((len(RELAYED),)),
                dma((len(LEFT_CUTS),)),
                dma((len(LEFT_CUTS),)),
                dma((2,)),
                dma((2,)),
                dma((2, STRUCTS)),
                dma((3, SLOTS)),
                dma((3, 2)),
                dma((3, 2)),
            ],
            compiler_params=pltpu.CompilerParams(
                collective_id=0, has_side_effects=True, vmem_limit_bytes=60 * 2**20
            ),
            cost_estimate=pl.CostEstimate(
                flops=2 * 1024 * 256 * 3072, bytes_accessed=2**20, transcendentals=8192
            ),
        )(momenta.T, spin_perm.T, spin_phase.T, left_modes, right_modes)

    placed = (P("mode", None, "space"), P("mode", None, "space"), P(), P(), P())
    return jax.shard_map(
        local, mesh=mesh, in_specs=placed, out_specs=P("space", "mode", None), check_vma=False
    )
```

```python
import math

import jax
import jax.numpy as jnp
from jax import lax
from jax.experimental import pallas as pl
from jax.experimental.pallas import tpu as pltpu
from jax.sharding import PartitionSpec as P

STRUCTS = 8
LAT = 96
BOX = 16
MODES = 64
COMP = 24
PAIRS = 12
SITES = 128
PARTS = 12
PER = PAIRS // PARTS
RELAYED = (8, 9, 10, 11)
LEFT_CUTS = ((0, 8), (8, 2), (10, 2))
NZ = 16
ROW = 8
SLOTS = 7
FLOAT = jnp.float32
HALF = jnp.bfloat16
MESH = pl.DeviceIdType.MESH


def kernel(
    momenta_hbm,
    perm_hbm,
    phase_hbm,
    left_hbm,
    right_hbm,
    out_ref,
    momenta,
    perm,
    phase,
    left_raw,
    right_raw,
    wide,
    angle,
    cosine,
    sine,
    left_own,
    left_far,
    right_own,
    right_far,
    relay,
    left_relay,
    rows,
    sums,
    send_one,
    take_one,
    send_two,
    take_two,
    load_sem,
    right_send,
    right_take,
    relay_take,
    relay_send,
    left_send,
    left_take,
    aside_take,
    aside_send,
    one_send,
    one_take,
    two_send,
    two_take,
):
    n_mode = lax.axis_size("mode")
    mode = lax.axis_index("mode")
    space = lax.axis_index("space")
    z = space // 2
    y = space % 2
    odd = z % 2
    in_row = lax.rem(mode, ROW)
    first_chip = in_row < 2
    last_chip = in_row >= ROW - 2

    def modes_on(step):
        return lax.rem(mode + step + n_mode, n_mode)

    def along(step):
        return lax.rem(z + step + NZ, NZ)

    loads = [
        pltpu.make_async_copy(source, target, load_sem.at[index])
        for index, (source, target) in enumerate(
            (
                (right_hbm, right_raw),
                (left_hbm, left_raw),
                (momenta_hbm, momenta),
                (perm_hbm, perm),
                (phase_hbm, phase),
            )
        )
    ]
    barrier = pltpu.get_barrier_semaphore()

    def greet(to_mode, to_space):
        pl.semaphore_signal(barrier, inc=1, device_id=(to_mode, to_space), device_id_type=MESH)

    for step in (5, -5, 0):
        if step == 0:

            @pl.when(y == 1)
            def _():
                greet(modes_on(0 - y), z * 2)
        else:
            greet(modes_on(0 - y), along(step) * 2)
        greet(modes_on(0 - y), along(step) * 2 + 1)

    for load in loads:
        load.start()

    for step in (3, -3, -2, 2, -1, 1):
        greet(mode, along(step) * 2 + y)

    greet(modes_on(-2), space)
    greet(modes_on(1), space)

    @pl.when(first_chip)
    def _():
        greet(mode + ROW - 2, space)
        greet(modes_on(-ROW), space)

    @pl.when(in_row == ROW - 1)
    def _():
        greet(mode - ROW + 1, space)
        greet(modes_on(ROW), space)

    def spread(raw):
        def step(part, carry):
            piece = raw[pl.ds(part * 8, 8)].astype(FLOAT).reshape(8 * COMP, SITES)
            wide[pl.ds(pl.multiple_of(part * 8 * COMP, 8 * COMP), 8 * COMP), :] = piece
            return carry

        lax.fori_loop(0, MODES // 8, step, 0)

    def component(index):
        return wide[pl.ds(index, MODES, stride=COMP), :]

    loads[0].wait()
    spread(right_raw)
    for pair in range(PAIRS):
        real, imag = component(pair), component(PAIRS + pair)
        right_own[pair, :MODES, :SITES] = real.astype(HALF)
        right_own[pair, :MODES, SITES:] = imag.astype(HALF)
        right_own[pair, MODES:, :SITES] = imag.astype(HALF)
        right_own[pair, MODES:, SITES:] = (-real).astype(HALF)
    loads[1].wait()
    spread(left_raw)
    for pair in range(PAIRS):
        left_own[pair, :, :SITES] = component(pair).astype(HALF)
        left_own[pair, :, SITES:] = component(PAIRS + pair).astype(HALF)

    edge = jnp.logical_or(first_chip, last_chip)
    ends = jnp.logical_or(in_row == 0, in_row == ROW - 1)
    pl.semaphore_wait(barrier, 13 + y + edge.astype(jnp.int32) + ends.astype(jnp.int32))

    def part_of(ref, part):
        return ref.at[pl.ds(part * PER, PER), pl.ds(0, MODES)]

    def right_copy(part):
        return pltpu.make_async_remote_copy(
            part_of(right_own, part),
            part_of(right_far, part),
            right_send.at[part],
            right_take.at[part],
            (modes_on(2), space),
            MESH,
        )

    def aside_copy(turn):
        return pltpu.make_async_remote_copy(
            part_of(right_own, RELAYED[turn]),
            relay.at[turn],
            right_send.at[RELAYED[turn]],
            relay_take.at[turn],
            (modes_on(2 - ROW), space),
            MESH,
        )

    def relay_copy(turn):
        return pltpu.make_async_remote_copy(
            relay.at[turn],
            part_of(right_far, RELAYED[turn]),
            relay_send.at[turn],
            right_take.at[RELAYED[turn]],
            (modes_on(ROW), space),
            MESH,
        )

    def left_part(ref, cut):
        start, size = LEFT_CUTS[cut]
        return ref.at[pl.ds(start, size)]

    def left_copy(cut):
        return pltpu.make_async_remote_copy(
            left_part(left_own, cut),
            left_part(left_far, cut),
            left_send.at[cut],
            left_take.at[cut],
            (modes_on(-1), space),
            MESH,
        )

    def left_aside(cut):
        return pltpu.make_async_remote_copy(
            left_part(left_own, cut),
            left_relay.at[cut - 1],
            left_send.at[cut],
            aside_take.at[cut - 1],
            (modes_on(ROW - 1), space),
            MESH,
        )

    def left_on(cut):
        return pltpu.make_async_remote_copy(
            left_relay.at[cut - 1],
            left_part(left_far, cut),
            aside_send.at[cut - 1],
            left_take.at[cut],
            (modes_on(-ROW), space),
            MESH,
        )

    def start_aside(turn):
        @pl.when(last_chip)
        def _():
            aside_copy(turn).start()

    start_aside(0)

    @pl.when(in_row == 0)
    def _():
        left_aside(1).start()
        left_aside(2).start()

    left_copy(0).start()

    @pl.when(in_row != 0)
    def _():
        left_copy(1).start()
        left_copy(2).start()

    for part in range(PARTS):
        if part not in RELAYED:
            right_copy(part).start()

    @pl.when(jnp.logical_not(last_chip))
    def _():
        for part in RELAYED:
            right_copy(part).start()

    start_aside(1)
    for load in loads[2:]:
        load.wait()

    lane = lax.broadcasted_iota(jnp.int32, (1, SITES), 1)
    first = lane % BOX
    second = (space * (SITES // BOX) + lane // BOX) % BOX
    third = space * SITES // (BOX * BOX)
    sources = []
    for struct in range(STRUCTS):
        dot = momenta[0, struct] * first + momenta[1, struct] * second + momenta[2, struct] * third
        own = []
        for spin in range(4):
            origin = jnp.int32(0)
            for other in range(1, 4):
                origin = jnp.where(perm[other, struct] == spin, other, origin)
            turn = phase[0, struct]
            for other in range(1, 4):
                turn = jnp.where(origin == other, phase[other, struct], turn)
            value = LAT // 4 * turn - dot + 2 * LAT
            quarter = value
            for times in range(1, 5):
                quarter = quarter - jnp.where(value >= times * LAT, LAT, 0)
            angle[pl.ds(struct * 4 + spin, 1), :] = quarter.astype(FLOAT) * (2.0 * math.pi / LAT)
            own.append(origin)
        sources.append(own)
        if struct % 4 == 3:
            start_aside(2 + struct // 4)
    cosine[...] = jnp.cos(angle[...])
    sine[...] = jnp.sin(angle[...])

    def turn_rows(li, structs):
        for struct in structs:
            for spin in range(4):
                origin = sources[struct][spin]
                turn_re = cosine[pl.ds(struct * 4 + spin, 1), :]
                turn_im = sine[pl.ds(struct * 4 + spin, 1), :]
                for colour in range(3):
                    block = (left_own, left_far)[li][origin * 3 + colour]
                    real = block[:, :SITES].astype(FLOAT)
                    imag = block[:, SITES:].astype(FLOAT)
                    place = rows.at[spin * 3 + colour, li, struct]
                    place[:, :SITES] = (real * turn_re + imag * turn_im).astype(HALF)
                    place[:, SITES:] = (imag * turn_re - real * turn_im).astype(HALF)

    def product(blocks, right, pairs):
        total = None
        for pair in pairs:
            left = jnp.concatenate(
                [rows[pair, li, a:b].reshape((b - a) * MODES, 2 * SITES) for li, a, b in blocks], axis=0
            )
            term = lax.dot_general(
                left, right[pair], (((1,), (1,)), ((), ())), preferred_element_type=FLOAT
            )
            total = term if total is None else total + term
        return total.reshape(-1, MODES, 2 * MODES)

    def near_sums(li):
        total = product([(li, 0, STRUCTS)], right_own, range(PAIRS))
        sums[0, li] = total
        for struct in range(STRUCTS):
            send_one[0, struct, li] = total[struct].astype(HALF)

    def far_arrive(parts):
        for part in parts:
            right_copy(part).wait_recv()
            for pair in range(part * PER, part * PER + PER):
                block = right_far[pair, :MODES, :]
                right_far[pair, MODES:, :SITES] = block[:, SITES:]
                right_far[pair, MODES:, SITES:] = (-block[:, :SITES].astype(FLOAT)).astype(HALF)

    def far_sums(li, pairs, fresh):
        total = product([(li, 0, STRUCTS)], right_far, pairs)
        sums[1, li] = total if fresh else sums[1, li] + total

    def one_place(rj, struct):
        to = 2 * struct + rj
        gap = lax.rem(z - to + NZ, NZ)
        middle = 8 if to < NZ // 2 else 7
        plus = jnp.logical_and(gap >= 3, gap <= middle)
        minus = jnp.logical_and(gap > middle, gap <= 13)
        role = jnp.where(plus, 1, jnp.where(minus, 2, 0))
        adder = lax.rem(to + jnp.where(plus, 5, jnp.where(minus, NZ - 5, 0)), NZ)
        slot = lax.rem(z - adder + NZ + 3, NZ)
        return adder, role, slot

    def one_copy(rj, struct):
        adder, role, slot = one_place(rj, struct)
        return adder != z, pltpu.make_async_remote_copy(
            send_one.at[rj, struct],
            take_one.at[role, slot],
            one_send.at[rj, struct],
            one_take.at[role, slot],
            (mode, adder * 2 + y),
            MESH,
        )

    def send_sums(rj, struct):
        away, copy = one_copy(rj, struct)

        @pl.when(away)
        def _():
            copy.start()

    def owner_z(role):
        return along((0, -5, 5)[role])

    def two_copy(role, li):
        return pltpu.make_async_remote_copy(
            send_two.at[role, li],
            take_two.at[role, y],
            two_send.at[role, li],
            two_take.at[role, y],
            (modes_on(li), owner_z(role) * 2 + li),
            MESH,
        )

    def add_and_pass(role):
        slots = (1, 2, 4, 5)
        if role == 0:
            add_slots(role, slots)
            return
        low = owner_z(role) < NZ // 2
        more = low if role == 1 else jnp.logical_not(low)

        @pl.when(more)
        def _():
            add_slots(role, slots + ((6,) if role == 1 else (0,)))

        @pl.when(jnp.logical_not(more))
        def _():
            add_slots(role, slots)

    def add_slots(role, slots):
        for slot in slots:
            pltpu.make_async_remote_copy(
                send_one.at[0, 0],
                take_one.at[role, slot],
                one_send.at[0, 0],
                one_take.at[role, slot],
                (mode, space),
                MESH,
            ).wait_recv()
        to = owner_z(role)
        for li in range(2):
            total = sums[to % 2, li, to // 2]
            for slot in slots:
                total = total + take_one[role, slot, li].astype(FLOAT)
            send_two[role, li] = total.astype(HALF)
            if role == 0 and li == 0:

                @pl.when(y == 0)
                def _():
                    take_two[0, 0] = total.astype(HALF)

                @pl.when(y == 1)
                def _():
                    two_copy(role, li).start()
            else:
                two_copy(role, li).start()

    def pass_sums(rj):
        @pl.when(odd == rj)
        def _():
            add_and_pass(0)

        @pl.when(odd != rj)
        def _():
            back = jnp.logical_and(z >= 5, z < 11)

            @pl.when(back)
            def _():
                add_and_pass(1)

            add_and_pass(2)

            @pl.when(jnp.logical_not(back))
            def _():
                add_and_pass(1)

    def hand_on(turn):
        @pl.when(first_chip)
        def _():
            aside_copy(turn).wait_recv()
            relay_copy(turn).start()

    def left_hand_on(cut):
        @pl.when(in_row == ROW - 1)
        def _():
            left_aside(cut).wait_recv()
            left_on(cut).start()

    turn_rows(0, range(0, 4))
    if len(RELAYED) > 4:
        start_aside(4)
    turn_rows(0, range(4, STRUCTS))
    if len(RELAYED) > 5:
        start_aside(5)
    hand_on(0)
    hand_on(1)
    left_hand_on(1)
    near_sums(0)
    left_hand_on(2)
    for turn in range(2, len(RELAYED)):
        hand_on(turn)
    for cut in range(len(LEFT_CUTS)):
        left_copy(cut).wait_recv()
    turn_rows(1, range(STRUCTS))
    near_sums(1)
    for struct in range(STRUCTS):
        send_sums(0, struct)
    far_arrive(range(0, 6))
    for li in range(2):
        far_sums(li, range(0, 6), True)
    far_arrive(range(6, 10))
    for li in range(2):
        far_sums(li, range(6, 10), False)
    far_arrive(range(10, PARTS))
    for q in range(STRUCTS // 2):
        last = product([(0, 2 * q, 2 * q + 2), (1, 2 * q, 2 * q + 2)], right_far, range(10, PAIRS))
        for struct in (2 * q, 2 * q + 1):
            for li in range(2):
                total = sums[1, li, struct] + last[2 * li + struct % 2]
                sums[1, li, struct] = total
                send_one[1, struct, li] = total.astype(HALF)
            send_sums(1, struct)
    pass_sums(0)
    pass_sums(1)

    total = jnp.zeros((MODES, 2 * MODES), FLOAT)
    for role in range(3):
        for from_y in range(2):
            arrived = pltpu.make_async_remote_copy(
                send_two.at[0, 0],
                take_two.at[role, from_y],
                two_send.at[0, 0],
                two_take.at[role, from_y],
                (mode, space),
                MESH,
            )
            if role == 0 and from_y == 0:

                @pl.when(y == 1)
                def _():
                    arrived.wait_recv()
            else:
                arrived.wait_recv()
            total = total + take_two[role, from_y].astype(FLOAT)
    total = total * (1.0 / math.sqrt(COMP * SITES * NZ * 2))
    out_ref[0] = total[:, :MODES]
    out_ref[1] = total[:, MODES:]

    for cut in range(len(LEFT_CUTS)):
        left_copy(cut).wait_send()
    for part in range(PARTS):
        right_copy(part).wait_send()

    @pl.when(first_chip)
    def _():
        for turn in range(len(RELAYED)):
            relay_copy(turn).wait_send()

    @pl.when(in_row == ROW - 1)
    def _():
        for cut in (1, 2):
            left_on(cut).wait_send()

    for rj in range(2):
        for struct in range(STRUCTS):
            away, copy = one_copy(rj, struct)

            @pl.when(away)
            def _():
                copy.wait_send()

    for role in range(3):
        for li in range(2):
            if role == 0 and li == 0:

                @pl.when(y == 1)
                def _():
                    two_copy(role, li).wait_send()
            else:
                two_copy(role, li).wait_send()


def solution(mesh):
    def local(left_modes, right_modes, momenta, spin_perm, spin_phase):
        large = pl.BlockSpec(memory_space=pl.ANY)
        dma = pltpu.SemaphoreType.DMA
        return pl.pallas_call(
            kernel,
            out_shape=jax.ShapeDtypeStruct((2, MODES, MODES), FLOAT),
            in_specs=[large] * 5,
            out_specs=pl.BlockSpec(memory_space=pltpu.VMEM),
            scratch_shapes=[
                pltpu.SMEM((3, STRUCTS), jnp.int32),
                pltpu.SMEM((4, STRUCTS), jnp.int32),
                pltpu.SMEM((4, STRUCTS), jnp.int32),
                pltpu.VMEM((MODES, COMP, SITES), HALF),
                pltpu.VMEM((MODES, COMP, SITES), HALF),
                pltpu.VMEM((MODES * COMP, SITES), FLOAT),
                pltpu.VMEM((STRUCTS * 4, SITES), FLOAT),
                pltpu.VMEM((STRUCTS * 4, SITES), FLOAT),
                pltpu.VMEM((STRUCTS * 4, SITES), FLOAT),
                pltpu.VMEM((PAIRS, MODES, 2 * SITES), HALF),
                pltpu.VMEM((PAIRS, MODES, 2 * SITES), HALF),
                pltpu.VMEM((PAIRS, 2 * MODES, 2 * SITES), HALF),
                pltpu.VMEM((PAIRS, 2 * MODES, 2 * SITES), HALF),
                pltpu.VMEM((len(RELAYED), PER, MODES, 2 * SITES), HALF),
                pltpu.VMEM((2, 2, MODES, 2 * SITES), HALF),
                pltpu.VMEM((PAIRS, 2, STRUCTS, MODES, 2 * SITES), HALF),
                pltpu.VMEM((2, 2, STRUCTS, MODES, 2 * MODES), FLOAT),
                pltpu.VMEM((2, STRUCTS, 2, MODES, 2 * MODES), HALF),
                pltpu.VMEM((3, SLOTS, 2, MODES, 2 * MODES), HALF),
                pltpu.VMEM((3, 2, MODES, 2 * MODES), HALF),
                pltpu.VMEM((3, 2, MODES, 2 * MODES), HALF),
                dma((5,)),
                dma((PARTS,)),
                dma((PARTS,)),
                dma((len(RELAYED),)),
                dma((len(RELAYED),)),
                dma((len(LEFT_CUTS),)),
                dma((len(LEFT_CUTS),)),
                dma((2,)),
                dma((2,)),
                dma((2, STRUCTS)),
                dma((3, SLOTS)),
                dma((3, 2)),
                dma((3, 2)),
            ],
            compiler_params=pltpu.CompilerParams(
                collective_id=0, has_side_effects=True, vmem_limit_bytes=60 * 2**20
            ),
            cost_estimate=pl.CostEstimate(
                flops=2 * 1024 * 256 * 3072, bytes_accessed=2**20, transcendentals=8192
            ),
        )(momenta.T, spin_perm.T, spin_phase.T, left_modes, right_modes)

    placed = (P("mode", None, "space"), P("mode", None, "space"), P(), P(), P())
    return jax.shard_map(
        local, mesh=mesh, in_specs=placed, out_specs=P("space", "mode", None), check_vma=False
    )
```

```python
import math

import jax
import jax.numpy as jnp
from jax import lax
from jax.experimental import pallas as pl
from jax.experimental.pallas import tpu as pltpu
from jax.sharding import PartitionSpec as P

STRUCTS = 8
LAT = 96
BOX = 16
MODES = 64
COMP = 24
PAIRS = 12
SITES = 128
PARTS = 12
PER = PAIRS // PARTS
RELAYED = (8, 9, 10, 11)
LEFT_CUTS = ((0, 8), (8, 2), (10, 2))
NZ = 16
ROW = 8
SLOTS = 7
FLOAT = jnp.float32
HALF = jnp.bfloat16
MESH = pl.DeviceIdType.MESH


def kernel(
    momenta_hbm,
    perm_hbm,
    phase_hbm,
    left_hbm,
    right_hbm,
    out_ref,
    momenta,
    perm,
    phase,
    left_raw,
    right_raw,
    wide,
    angle,
    cosine,
    sine,
    left_own,
    left_far,
    right_own,
    right_far,
    relay,
    left_relay,
    rows,
    sums,
    send_one,
    take_one,
    send_two,
    take_two,
    load_sem,
    right_send,
    right_take,
    relay_take,
    relay_send,
    left_send,
    left_take,
    aside_take,
    aside_send,
    one_send,
    one_take,
    two_send,
    two_take,
):
    n_mode = lax.axis_size("mode")
    mode = lax.axis_index("mode")
    space = lax.axis_index("space")
    z = space // 2
    y = space % 2
    odd = z % 2
    in_row = lax.rem(mode, ROW)
    first_chip = in_row < 2
    last_chip = in_row >= ROW - 2

    def modes_on(step):
        return lax.rem(mode + step + n_mode, n_mode)

    def along(step):
        return lax.rem(z + step + NZ, NZ)

    loads = [
        pltpu.make_async_copy(source, target, load_sem.at[index])
        for index, (source, target) in enumerate(
            (
                (right_hbm, right_raw),
                (left_hbm, left_raw),
                (momenta_hbm, momenta),
                (perm_hbm, perm),
                (phase_hbm, phase),
            )
        )
    ]
    barrier = pltpu.get_barrier_semaphore()

    def greet(to_mode, to_space):
        pl.semaphore_signal(barrier, inc=1, device_id=(to_mode, to_space), device_id_type=MESH)

    for step in (5, -5, 0):
        if step == 0:

            @pl.when(y == 1)
            def _():
                greet(modes_on(0 - y), z * 2)
        else:
            greet(modes_on(0 - y), along(step) * 2)
        greet(modes_on(0 - y), along(step) * 2 + 1)

    for load in loads:
        load.start()

    for step in (3, -3, -2, 2, -1, 1):
        greet(mode, along(step) * 2 + y)

    greet(modes_on(-2), space)
    greet(modes_on(1), space)

    @pl.when(first_chip)
    def _():
        greet(mode + ROW - 2, space)
        greet(modes_on(-ROW), space)

    @pl.when(in_row == ROW - 1)
    def _():
        greet(mode - ROW + 1, space)
        greet(modes_on(ROW), space)

    def spread(raw):
        def step(part, carry):
            piece = raw[pl.ds(part * 8, 8)].astype(FLOAT).reshape(8 * COMP, SITES)
            wide[pl.ds(pl.multiple_of(part * 8 * COMP, 8 * COMP), 8 * COMP), :] = piece
            return carry

        lax.fori_loop(0, MODES // 8, step, 0)

    def component(index):
        return wide[pl.ds(index, MODES, stride=COMP), :]

    loads[0].wait()
    spread(right_raw)
    for pair in range(PAIRS):
        real, imag = component(pair), component(PAIRS + pair)
        right_own[pair, :MODES, :SITES] = real.astype(HALF)
        right_own[pair, :MODES, SITES:] = imag.astype(HALF)
        right_own[pair, MODES:, :SITES] = imag.astype(HALF)
        right_own[pair, MODES:, SITES:] = (-real).astype(HALF)
    loads[1].wait()
    spread(left_raw)
    for pair in range(PAIRS):
        left_own[pair, :, :SITES] = component(pair).astype(HALF)
        left_own[pair, :, SITES:] = component(PAIRS + pair).astype(HALF)

    edge = jnp.logical_or(first_chip, last_chip)
    ends = jnp.logical_or(in_row == 0, in_row == ROW - 1)
    pl.semaphore_wait(barrier, 13 + y + edge.astype(jnp.int32) + ends.astype(jnp.int32))

    def part_of(ref, part):
        return ref.at[pl.ds(part * PER, PER), pl.ds(0, MODES)]

    def right_copy(part):
        return pltpu.make_async_remote_copy(
            part_of(right_own, part),
            part_of(right_far, part),
            right_send.at[part],
            right_take.at[part],
            (modes_on(2), space),
            MESH,
        )

    def aside_copy(turn):
        return pltpu.make_async_remote_copy(
            part_of(right_own, RELAYED[turn]),
            relay.at[turn],
            right_send.at[RELAYED[turn]],
            relay_take.at[turn],
            (modes_on(2 - ROW), space),
            MESH,
        )

    def relay_copy(turn):
        return pltpu.make_async_remote_copy(
            relay.at[turn],
            part_of(right_far, RELAYED[turn]),
            relay_send.at[turn],
            right_take.at[RELAYED[turn]],
            (modes_on(ROW), space),
            MESH,
        )

    def left_part(ref, cut):
        start, size = LEFT_CUTS[cut]
        return ref.at[pl.ds(start, size)]

    def left_copy(cut):
        return pltpu.make_async_remote_copy(
            left_part(left_own, cut),
            left_part(left_far, cut),
            left_send.at[cut],
            left_take.at[cut],
            (modes_on(-1), space),
            MESH,
        )

    def left_aside(cut):
        return pltpu.make_async_remote_copy(
            left_part(left_own, cut),
            left_relay.at[cut - 1],
            left_send.at[cut],
            aside_take.at[cut - 1],
            (modes_on(ROW - 1), space),
            MESH,
        )

    def left_on(cut):
        return pltpu.make_async_remote_copy(
            left_relay.at[cut - 1],
            left_part(left_far, cut),
            aside_send.at[cut - 1],
            left_take.at[cut],
            (modes_on(-ROW), space),
            MESH,
        )

    def start_aside(turn):
        @pl.when(last_chip)
        def _():
            aside_copy(turn).start()

    start_aside(0)

    @pl.when(in_row == 0)
    def _():
        left_aside(1).start()
        left_aside(2).start()

    left_copy(0).start()

    @pl.when(in_row != 0)
    def _():
        left_copy(1).start()
        left_copy(2).start()

    for part in range(PARTS):
        if part not in RELAYED:
            right_copy(part).start()

    @pl.when(jnp.logical_not(last_chip))
    def _():
        for part in RELAYED:
            right_copy(part).start()

    start_aside(1)
    for load in loads[2:]:
        load.wait()

    lane = lax.broadcasted_iota(jnp.int32, (1, SITES), 1)
    first = lane % BOX
    second = (space * (SITES // BOX) + lane // BOX) % BOX
    third = space * SITES // (BOX * BOX)
    sources = []
    for struct in range(STRUCTS):
        dot = momenta[0, struct] * first + momenta[1, struct] * second + momenta[2, struct] * third
        own = []
        for spin in range(4):
            origin = jnp.int32(0)
            for other in range(1, 4):
                origin = jnp.where(perm[other, struct] == spin, other, origin)
            turn = phase[0, struct]
            for other in range(1, 4):
                turn = jnp.where(origin == other, phase[other, struct], turn)
            value = LAT // 4 * turn - dot + 2 * LAT
            quarter = value
            for times in range(1, 5):
                quarter = quarter - jnp.where(value >= times * LAT, LAT, 0)
            angle[pl.ds(struct * 4 + spin, 1), :] = quarter.astype(FLOAT) * (2.0 * math.pi / LAT)
            own.append(origin)
        sources.append(own)
        if struct % 4 == 3:
            start_aside(2 + struct // 4)
    cosine[...] = jnp.cos(angle[...])
    sine[...] = jnp.sin(angle[...])

    def turn_rows(li, structs):
        for struct in structs:
            for spin in range(4):
                origin = sources[struct][spin]
                turn_re = cosine[pl.ds(struct * 4 + spin, 1), :]
                turn_im = sine[pl.ds(struct * 4 + spin, 1), :]
                for colour in range(3):
                    block = (left_own, left_far)[li][origin * 3 + colour]
                    real = block[:, :SITES].astype(FLOAT)
                    imag = block[:, SITES:].astype(FLOAT)
                    place = rows.at[spin * 3 + colour, li, struct]
                    place[:, :SITES] = (real * turn_re + imag * turn_im).astype(HALF)
                    place[:, SITES:] = (imag * turn_re - real * turn_im).astype(HALF)

    def product(blocks, right, pairs):
        total = None
        for pair in pairs:
            left = jnp.concatenate(
                [rows[pair, li, a:b].reshape((b - a) * MODES, 2 * SITES) for li, a, b in blocks], axis=0
            )
            term = lax.dot_general(
                left, right[pair], (((1,), (1,)), ((), ())), preferred_element_type=FLOAT
            )
            total = term if total is None else total + term
        return total.reshape(-1, MODES, 2 * MODES)

    def near_sums(li):
        total = product([(li, 0, STRUCTS)], right_own, range(PAIRS))
        sums[0, li] = total
        for struct in range(STRUCTS):
            send_one[0, struct, li] = total[struct].astype(HALF)

    def far_arrive(parts):
        for part in parts:
            right_copy(part).wait_recv()
            for pair in range(part * PER, part * PER + PER):
                block = right_far[pair, :MODES, :]
                right_far[pair, MODES:, :SITES] = block[:, SITES:]
                right_far[pair, MODES:, SITES:] = (-block[:, :SITES].astype(FLOAT)).astype(HALF)

    def far_sums(li, pairs, fresh):
        total = product([(li, 0, STRUCTS)], right_far, pairs)
        sums[1, li] = total if fresh else sums[1, li] + total

    def one_place(rj, struct):
        to = 2 * struct + rj
        gap = lax.rem(z - to + NZ, NZ)
        middle = 8 if to < NZ // 2 else 7
        plus = jnp.logical_and(gap >= 3, gap <= middle)
        minus = jnp.logical_and(gap > middle, gap <= 13)
        role = jnp.where(plus, 1, jnp.where(minus, 2, 0))
        adder = lax.rem(to + jnp.where(plus, 5, jnp.where(minus, NZ - 5, 0)), NZ)
        slot = lax.rem(z - adder + NZ + 3, NZ)
        return adder, role, slot

    def one_copy(rj, struct):
        adder, role, slot = one_place(rj, struct)
        return adder != z, pltpu.make_async_remote_copy(
            send_one.at[rj, struct],
            take_one.at[role, slot],
            one_send.at[rj, struct],
            one_take.at[role, slot],
            (mode, adder * 2 + y),
            MESH,
        )

    def send_sums(rj, struct):
        away, copy = one_copy(rj, struct)

        @pl.when(away)
        def _():
            copy.start()

    def owner_z(role):
        return along((0, -5, 5)[role])

    def two_copy(role, li):
        return pltpu.make_async_remote_copy(
            send_two.at[role, li],
            take_two.at[role, y],
            two_send.at[role, li],
            two_take.at[role, y],
            (modes_on(li), owner_z(role) * 2 + li),
            MESH,
        )

    def add_and_pass(role):
        slots = (1, 2, 4, 5)
        if role == 0:
            add_slots(role, slots)
            return
        low = owner_z(role) < NZ // 2
        more = low if role == 1 else jnp.logical_not(low)

        @pl.when(more)
        def _():
            add_slots(role, slots + ((6,) if role == 1 else (0,)))

        @pl.when(jnp.logical_not(more))
        def _():
            add_slots(role, slots)

    def add_slots(role, slots):
        for slot in slots:
            pltpu.make_async_remote_copy(
                send_one.at[0, 0],
                take_one.at[role, slot],
                one_send.at[0, 0],
                one_take.at[role, slot],
                (mode, space),
                MESH,
            ).wait_recv()
        to = owner_z(role)
        for li in range(2):
            total = sums[to % 2, li, to // 2]
            for slot in slots:
                total = total + take_one[role, slot, li].astype(FLOAT)
            send_two[role, li] = total.astype(HALF)
            if role == 0 and li == 0:

                @pl.when(y == 0)
                def _():
                    take_two[0, 0] = total.astype(HALF)

                @pl.when(y == 1)
                def _():
                    two_copy(role, li).start()
            else:
                two_copy(role, li).start()

    def pass_sums(rj):
        @pl.when(odd == rj)
        def _():
            add_and_pass(0)

        @pl.when(odd != rj)
        def _():
            back = jnp.logical_and(z >= 5, z < 11)

            @pl.when(back)
            def _():
                add_and_pass(1)

            add_and_pass(2)

            @pl.when(jnp.logical_not(back))
            def _():
                add_and_pass(1)

    def hand_on(turn):
        @pl.when(first_chip)
        def _():
            aside_copy(turn).wait_recv()
            relay_copy(turn).start()

    def left_hand_on(cut):
        @pl.when(in_row == ROW - 1)
        def _():
            left_aside(cut).wait_recv()
            left_on(cut).start()

    turn_rows(0, range(0, 4))
    if len(RELAYED) > 4:
        start_aside(4)
    turn_rows(0, range(4, STRUCTS))
    if len(RELAYED) > 5:
        start_aside(5)
    hand_on(0)
    hand_on(1)
    left_hand_on(1)
    near_sums(0)
    left_hand_on(2)
    for turn in range(2, len(RELAYED)):
        hand_on(turn)
    for cut in range(len(LEFT_CUTS)):
        left_copy(cut).wait_recv()
    turn_rows(1, range(STRUCTS))
    near_sums(1)
    for struct in range(STRUCTS):
        send_sums(0, struct)
    far_arrive(range(0, 6))
    for li in range(2):
        far_sums(li, range(0, 6), True)
    far_arrive(range(6, 10))
    for li in range(2):
        far_sums(li, range(6, 10), False)
    far_arrive(range(10, PARTS))
    for q in range(STRUCTS // 2):
        last = product([(0, 2 * q, 2 * q + 2), (1, 2 * q, 2 * q + 2)], right_far, range(10, PAIRS))
        for struct in (2 * q, 2 * q + 1):
            for li in range(2):
                total = sums[1, li, struct] + last[2 * li + struct % 2]
                sums[1, li, struct] = total
                send_one[1, struct, li] = total.astype(HALF)
            send_sums(1, struct)
    pass_sums(0)
    pass_sums(1)

    total = jnp.zeros((MODES, 2 * MODES), FLOAT)
    for role in range(3):
        for from_y in range(2):
            arrived = pltpu.make_async_remote_copy(
                send_two.at[0, 0],
                take_two.at[role, from_y],
                two_send.at[0, 0],
                two_take.at[role, from_y],
                (mode, space),
                MESH,
            )
            if role == 0 and from_y == 0:

                @pl.when(y == 1)
                def _():
                    arrived.wait_recv()
            else:
                arrived.wait_recv()
            total = total + take_two[role, from_y].astype(FLOAT)
    total = total * (1.0 / math.sqrt(COMP * SITES * NZ * 2))
    out_ref[0] = total[:, :MODES]
    out_ref[1] = total[:, MODES:]

    for cut in range(len(LEFT_CUTS)):
        left_copy(cut).wait_send()
    for part in range(PARTS):
        right_copy(part).wait_send()

    @pl.when(first_chip)
    def _():
        for turn in range(len(RELAYED)):
            relay_copy(turn).wait_send()

    @pl.when(in_row == ROW - 1)
    def _():
        for cut in (1, 2):
            left_on(cut).wait_send()

    for rj in range(2):
        for struct in range(STRUCTS):
            away, copy = one_copy(rj, struct)

            @pl.when(away)
            def _():
                copy.wait_send()

    for role in range(3):
        for li in range(2):
            if role == 0 and li == 0:

                @pl.when(y == 1)
                def _():
                    two_copy(role, li).wait_send()
            else:
                two_copy(role, li).wait_send()


def solution(mesh):
    def local(left_modes, right_modes, momenta, spin_perm, spin_phase):
        large = pl.BlockSpec(memory_space=pl.ANY)
        dma = pltpu.SemaphoreType.DMA
        return pl.pallas_call(
            kernel,
            out_shape=jax.ShapeDtypeStruct((2, MODES, MODES), FLOAT),
            in_specs=[large] * 5,
            out_specs=pl.BlockSpec(memory_space=pltpu.VMEM),
            scratch_shapes=[
                pltpu.SMEM((3, STRUCTS), jnp.int32),
                pltpu.SMEM((4, STRUCTS), jnp.int32),
                pltpu.SMEM((4, STRUCTS), jnp.int32),
                pltpu.VMEM((MODES, COMP, SITES), HALF),
                pltpu.VMEM((MODES, COMP, SITES), HALF),
                pltpu.VMEM((MODES * COMP, SITES), FLOAT),
                pltpu.VMEM((STRUCTS * 4, SITES), FLOAT),
                pltpu.VMEM((STRUCTS * 4, SITES), FLOAT),
                pltpu.VMEM((STRUCTS * 4, SITES), FLOAT),
                pltpu.VMEM((PAIRS, MODES, 2 * SITES), HALF),
                pltpu.VMEM((PAIRS, MODES, 2 * SITES), HALF),
                pltpu.VMEM((PAIRS, 2 * MODES, 2 * SITES), HALF),
                pltpu.VMEM((PAIRS, 2 * MODES, 2 * SITES), HALF),
                pltpu.VMEM((len(RELAYED), PER, MODES, 2 * SITES), HALF),
                pltpu.VMEM((2, 2, MODES, 2 * SITES), HALF),
                pltpu.VMEM((PAIRS, 2, STRUCTS, MODES, 2 * SITES), HALF),
                pltpu.VMEM((2, 2, STRUCTS, MODES, 2 * MODES), FLOAT),
                pltpu.VMEM((2, STRUCTS, 2, MODES, 2 * MODES), HALF),
                pltpu.VMEM((3, SLOTS, 2, MODES, 2 * MODES), HALF),
                pltpu.VMEM((3, 2, MODES, 2 * MODES), HALF),
                pltpu.VMEM((3, 2, MODES, 2 * MODES), HALF),
                dma((5,)),
                dma((PARTS,)),
                dma((PARTS,)),
                dma((len(RELAYED),)),
                dma((len(RELAYED),)),
                dma((len(LEFT_CUTS),)),
                dma((len(LEFT_CUTS),)),
                dma((2,)),
                dma((2,)),
                dma((2, STRUCTS)),
                dma((3, SLOTS)),
                dma((3, 2)),
                dma((3, 2)),
            ],
            compiler_params=pltpu.CompilerParams(
                collective_id=0, has_side_effects=True, vmem_limit_bytes=40 * 2**20
            ),
            cost_estimate=pl.CostEstimate(
                flops=2 * 1024 * 256 * 3072, bytes_accessed=2**20, transcendentals=8192
            ),
        )(
            *(
                pltpu.with_memory_space_constraint(array, pltpu.HBM)
                for array in (momenta.T, spin_perm.T, spin_phase.T, left_modes, right_modes)
            )
        )

    placed = (P("mode", None, "space"), P("mode", None, "space"), P(), P(), P())
    return jax.shard_map(
        local, mesh=mesh, in_specs=placed, out_specs=P("space", "mode", None), check_vma=False
    )
```

```python
import math

import jax
import jax.numpy as jnp
from jax import lax
from jax.experimental import pallas as pl
from jax.experimental.pallas import tpu as pltpu
from jax.sharding import PartitionSpec as P

STRUCTS = 8
LAT = 96
BOX = 16
MODES = 64
COMP = 24
PAIRS = 12
SITES = 128
PARTS = 12
PER = PAIRS // PARTS
RELAYED = (8, 9, 10, 11)
LEFT_CUTS = ((0, 8), (8, 2), (10, 2))
NZ = 16
ROW = 8
SLOTS = 7
FLOAT = jnp.float32
HALF = jnp.bfloat16
MESH = pl.DeviceIdType.MESH


def kernel(
    momenta_hbm,
    perm_hbm,
    phase_hbm,
    left_hbm,
    right_hbm,
    out_ref,
    momenta,
    perm,
    phase,
    left_raw,
    right_raw,
    wide,
    angle,
    cosine,
    sine,
    left_own,
    left_far,
    right_own,
    right_far,
    relay,
    left_relay,
    rows,
    sums,
    send_one,
    take_one,
    send_two,
    take_two,
    load_sem,
    right_send,
    right_take,
    relay_take,
    relay_send,
    left_send,
    left_take,
    aside_take,
    aside_send,
    one_send,
    one_take,
    two_send,
    two_take,
):
    n_mode = lax.axis_size("mode")
    mode = lax.axis_index("mode")
    space = lax.axis_index("space")
    z = space // 2
    y = space % 2
    odd = z % 2
    in_row = lax.rem(mode, ROW)
    first_chip = in_row < 2
    last_chip = in_row >= ROW - 2

    def modes_on(step):
        return lax.rem(mode + step + n_mode, n_mode)

    def along(step):
        return lax.rem(z + step + NZ, NZ)

    loads = [
        pltpu.make_async_copy(source, target, load_sem.at[index])
        for index, (source, target) in enumerate(
            (
                (right_hbm, right_raw),
                (left_hbm, left_raw),
                (momenta_hbm, momenta),
                (perm_hbm, perm),
                (phase_hbm, phase),
            )
        )
    ]
    barrier = pltpu.get_barrier_semaphore()

    def greet(to_mode, to_space):
        pl.semaphore_signal(barrier, inc=1, device_id=(to_mode, to_space), device_id_type=MESH)

    for step in (5, -5, 0):
        if step == 0:

            @pl.when(y == 1)
            def _():
                greet(modes_on(0 - y), z * 2)
        else:
            greet(modes_on(0 - y), along(step) * 2)
        greet(modes_on(0 - y), along(step) * 2 + 1)

    for load in loads:
        load.start()

    for step in (3, -3, -2, 2, -1, 1):
        greet(mode, along(step) * 2 + y)

    greet(modes_on(-2), space)
    greet(modes_on(1), space)

    @pl.when(first_chip)
    def _():
        greet(mode + ROW - 2, space)
        greet(modes_on(-ROW), space)

    @pl.when(in_row == ROW - 1)
    def _():
        greet(mode - ROW + 1, space)
        greet(modes_on(ROW), space)

    def spread(raw):
        def step(part, carry):
            piece = raw[pl.ds(part * 8, 8)].astype(FLOAT).reshape(8 * COMP, SITES)
            wide[pl.ds(pl.multiple_of(part * 8 * COMP, 8 * COMP), 8 * COMP), :] = piece
            return carry

        lax.fori_loop(0, MODES // 8, step, 0)

    def component(index):
        return wide[pl.ds(index, MODES, stride=COMP), :]

    loads[0].wait()
    spread(right_raw)
    for pair in range(PAIRS):
        real, imag = component(pair), component(PAIRS + pair)
        right_own[pair, :MODES, :SITES] = real.astype(HALF)
        right_own[pair, :MODES, SITES:] = imag.astype(HALF)
        right_own[pair, MODES:, :SITES] = imag.astype(HALF)
        right_own[pair, MODES:, SITES:] = (-real).astype(HALF)
    loads[1].wait()
    spread(left_raw)
    for pair in range(PAIRS):
        left_own[pair, :, :SITES] = component(pair).astype(HALF)
        left_own[pair, :, SITES:] = component(PAIRS + pair).astype(HALF)

    edge = jnp.logical_or(first_chip, last_chip)
    ends = jnp.logical_or(in_row == 0, in_row == ROW - 1)
    pl.semaphore_wait(barrier, 13 + y + edge.astype(jnp.int32) + ends.astype(jnp.int32))

    def part_of(ref, part):
        return ref.at[pl.ds(part * PER, PER), pl.ds(0, MODES)]

    def right_copy(part):
        return pltpu.make_async_remote_copy(
            part_of(right_own, part),
            part_of(right_far, part),
            right_send.at[part],
            right_take.at[part],
            (modes_on(2), space),
            MESH,
        )

    def aside_copy(turn):
        return pltpu.make_async_remote_copy(
            part_of(right_own, RELAYED[turn]),
            relay.at[turn],
            right_send.at[RELAYED[turn]],
            relay_take.at[turn],
            (modes_on(2 - ROW), space),
            MESH,
        )

    def relay_copy(turn):
        return pltpu.make_async_remote_copy(
            relay.at[turn],
            part_of(right_far, RELAYED[turn]),
            relay_send.at[turn],
            right_take.at[RELAYED[turn]],
            (modes_on(ROW), space),
            MESH,
        )

    def left_part(ref, cut):
        start, size = LEFT_CUTS[cut]
        return ref.at[pl.ds(start, size)]

    def left_copy(cut):
        return pltpu.make_async_remote_copy(
            left_part(left_own, cut),
            left_part(left_far, cut),
            left_send.at[cut],
            left_take.at[cut],
            (modes_on(-1), space),
            MESH,
        )

    def left_aside(cut):
        return pltpu.make_async_remote_copy(
            left_part(left_own, cut),
            left_relay.at[cut - 1],
            left_send.at[cut],
            aside_take.at[cut - 1],
            (modes_on(ROW - 1), space),
            MESH,
        )

    def left_on(cut):
        return pltpu.make_async_remote_copy(
            left_relay.at[cut - 1],
            left_part(left_far, cut),
            aside_send.at[cut - 1],
            left_take.at[cut],
            (modes_on(-ROW), space),
            MESH,
        )

    def start_aside(turn):
        @pl.when(last_chip)
        def _():
            aside_copy(turn).start()

    start_aside(0)

    @pl.when(in_row == 0)
    def _():
        left_aside(1).start()
        left_aside(2).start()

    left_copy(0).start()

    @pl.when(in_row != 0)
    def _():
        left_copy(1).start()
        left_copy(2).start()

    for part in range(PARTS):
        if part not in RELAYED:
            right_copy(part).start()

    @pl.when(jnp.logical_not(last_chip))
    def _():
        for part in RELAYED:
            right_copy(part).start()

    start_aside(1)
    for load in loads[2:]:
        load.wait()

    lane = lax.broadcasted_iota(jnp.int32, (1, SITES), 1)
    first = lane % BOX
    second = (space * (SITES // BOX) + lane // BOX) % BOX
    third = space * SITES // (BOX * BOX)
    sources = []
    for struct in range(STRUCTS):
        dot = momenta[0, struct] * first + momenta[1, struct] * second + momenta[2, struct] * third
        own = []
        for spin in range(4):
            origin = jnp.int32(0)
            for other in range(1, 4):
                origin = jnp.where(perm[other, struct] == spin, other, origin)
            turn = phase[0, struct]
            for other in range(1, 4):
                turn = jnp.where(origin == other, phase[other, struct], turn)
            value = LAT // 4 * turn - dot + 2 * LAT
            quarter = value
            for times in range(1, 5):
                quarter = quarter - jnp.where(value >= times * LAT, LAT, 0)
            angle[pl.ds(struct * 4 + spin, 1), :] = quarter.astype(FLOAT) * (2.0 * math.pi / LAT)
            own.append(origin)
        sources.append(own)
        if struct % 4 == 3:
            start_aside(2 + struct // 4)
    cosine[...] = jnp.cos(angle[...])
    sine[...] = jnp.sin(angle[...])

    def turn_rows(li, structs):
        for struct in structs:
            for spin in range(4):
                origin = sources[struct][spin]
                turn_re = cosine[pl.ds(struct * 4 + spin, 1), :]
                turn_im = sine[pl.ds(struct * 4 + spin, 1), :]
                for colour in range(3):
                    block = (left_own, left_far)[li][origin * 3 + colour]
                    real = block[:, :SITES].astype(FLOAT)
                    imag = block[:, SITES:].astype(FLOAT)
                    place = rows.at[spin * 3 + colour, li, struct]
                    place[:, :SITES] = (real * turn_re + imag * turn_im).astype(HALF)
                    place[:, SITES:] = (imag * turn_re - real * turn_im).astype(HALF)

    def product(blocks, right, pairs):
        total = None
        for pair in pairs:
            left = jnp.concatenate(
                [rows[pair, li, a:b].reshape((b - a) * MODES, 2 * SITES) for li, a, b in blocks], axis=0
            )
            term = lax.dot_general(
                left, right[pair], (((1,), (1,)), ((), ())), preferred_element_type=FLOAT
            )
            total = term if total is None else total + term
        return total.reshape(-1, MODES, 2 * MODES)

    def near_sums(li):
        total = product([(li, 0, STRUCTS)], right_own, range(PAIRS))
        sums[0, li] = total
        for struct in range(STRUCTS):
            send_one[0, struct, li] = total[struct].astype(HALF)

    def far_arrive(parts):
        for part in parts:
            right_copy(part).wait_recv()
            for pair in range(part * PER, part * PER + PER):
                block = right_far[pair, :MODES, :]
                right_far[pair, MODES:, :SITES] = block[:, SITES:]
                right_far[pair, MODES:, SITES:] = (-block[:, :SITES].astype(FLOAT)).astype(HALF)

    def far_sums(li, pairs, fresh):
        total = product([(li, 0, STRUCTS)], right_far, pairs)
        sums[1, li] = total if fresh else sums[1, li] + total

    def one_place(rj, struct):
        to = 2 * struct + rj
        gap = lax.rem(z - to + NZ, NZ)
        middle = 8 if to < NZ // 2 else 7
        plus = jnp.logical_and(gap >= 3, gap <= middle)
        minus = jnp.logical_and(gap > middle, gap <= 13)
        role = jnp.where(plus, 1, jnp.where(minus, 2, 0))
        adder = lax.rem(to + jnp.where(plus, 5, jnp.where(minus, NZ - 5, 0)), NZ)
        slot = lax.rem(z - adder + NZ + 3, NZ)
        return adder, role, slot

    def one_copy(rj, struct):
        adder, role, slot = one_place(rj, struct)
        return adder != z, pltpu.make_async_remote_copy(
            send_one.at[rj, struct],
            take_one.at[role, slot],
            one_send.at[rj, struct],
            one_take.at[role, slot],
            (mode, adder * 2 + y),
            MESH,
        )

    def send_sums(rj, struct):
        away, copy = one_copy(rj, struct)

        @pl.when(away)
        def _():
            copy.start()

    def owner_z(role):
        return along((0, -5, 5)[role])

    def two_copy(role, li):
        return pltpu.make_async_remote_copy(
            send_two.at[role, li],
            take_two.at[role, y],
            two_send.at[role, li],
            two_take.at[role, y],
            (modes_on(li), owner_z(role) * 2 + li),
            MESH,
        )

    def add_and_pass(role):
        slots = (1, 2, 4, 5)
        if role == 0:
            add_slots(role, slots)
            return
        low = owner_z(role) < NZ // 2
        more = low if role == 1 else jnp.logical_not(low)

        @pl.when(more)
        def _():
            add_slots(role, slots + ((6,) if role == 1 else (0,)))

        @pl.when(jnp.logical_not(more))
        def _():
            add_slots(role, slots)

    def add_slots(role, slots):
        for slot in slots:
            pltpu.make_async_remote_copy(
                send_one.at[0, 0],
                take_one.at[role, slot],
                one_send.at[0, 0],
                one_take.at[role, slot],
                (mode, space),
                MESH,
            ).wait_recv()
        to = owner_z(role)
        for li in range(2):
            total = sums[to % 2, li, to // 2]
            for slot in slots:
                total = total + take_one[role, slot, li].astype(FLOAT)
            send_two[role, li] = total.astype(HALF)
            if role == 0 and li == 0:

                @pl.when(y == 0)
                def _():
                    take_two[0, 0] = total.astype(HALF)

                @pl.when(y == 1)
                def _():
                    two_copy(role, li).start()
            else:
                two_copy(role, li).start()

    def pass_sums(rj):
        @pl.when(odd == rj)
        def _():
            add_and_pass(0)

        @pl.when(odd != rj)
        def _():
            back = jnp.logical_and(z >= 5, z < 11)

            @pl.when(back)
            def _():
                add_and_pass(1)

            add_and_pass(2)

            @pl.when(jnp.logical_not(back))
            def _():
                add_and_pass(1)

    def hand_on(turn):
        @pl.when(first_chip)
        def _():
            aside_copy(turn).wait_recv()
            relay_copy(turn).start()

    def left_hand_on(cut):
        @pl.when(in_row == ROW - 1)
        def _():
            left_aside(cut).wait_recv()
            left_on(cut).start()

    turn_rows(0, range(0, 4))
    if len(RELAYED) > 4:
        start_aside(4)
    turn_rows(0, range(4, STRUCTS))
    if len(RELAYED) > 5:
        start_aside(5)
    hand_on(0)
    hand_on(1)
    left_hand_on(1)
    left_hand_on(2)
    for turn in range(2, len(RELAYED)):
        hand_on(turn)
    near_sums(0)
    for cut in range(len(LEFT_CUTS)):
        left_copy(cut).wait_recv()
    turn_rows(1, range(STRUCTS))
    near_sums(1)
    for struct in range(STRUCTS):
        send_sums(0, struct)
    far_arrive(range(0, 6))
    for li in range(2):
        far_sums(li, range(0, 6), True)
    far_arrive(range(6, 10))
    for li in range(2):
        far_sums(li, range(6, 10), False)
    far_arrive(range(10, PARTS))
    for q in range(STRUCTS // 2):
        last = product([(0, 2 * q, 2 * q + 2), (1, 2 * q, 2 * q + 2)], right_far, range(10, PAIRS))
        for struct in (2 * q, 2 * q + 1):
            for li in range(2):
                total = sums[1, li, struct] + last[2 * li + struct % 2]
                sums[1, li, struct] = total
                send_one[1, struct, li] = total.astype(HALF)
            send_sums(1, struct)
    pass_sums(0)
    pass_sums(1)

    total = jnp.zeros((MODES, 2 * MODES), FLOAT)
    for role in range(3):
        for from_y in range(2):
            arrived = pltpu.make_async_remote_copy(
                send_two.at[0, 0],
                take_two.at[role, from_y],
                two_send.at[0, 0],
                two_take.at[role, from_y],
                (mode, space),
                MESH,
            )
            if role == 0 and from_y == 0:

                @pl.when(y == 1)
                def _():
                    arrived.wait_recv()
            else:
                arrived.wait_recv()
            total = total + take_two[role, from_y].astype(FLOAT)
    total = total * (1.0 / math.sqrt(COMP * SITES * NZ * 2))
    out_ref[0] = total[:, :MODES]
    out_ref[1] = total[:, MODES:]

    for cut in range(len(LEFT_CUTS)):
        left_copy(cut).wait_send()
    for part in range(PARTS):
        right_copy(part).wait_send()

    @pl.when(first_chip)
    def _():
        for turn in range(len(RELAYED)):
            relay_copy(turn).wait_send()

    @pl.when(in_row == ROW - 1)
    def _():
        for cut in (1, 2):
            left_on(cut).wait_send()

    for rj in range(2):
        for struct in range(STRUCTS):
            away, copy = one_copy(rj, struct)

            @pl.when(away)
            def _():
                copy.wait_send()

    for role in range(3):
        for li in range(2):
            if role == 0 and li == 0:

                @pl.when(y == 1)
                def _():
                    two_copy(role, li).wait_send()
            else:
                two_copy(role, li).wait_send()


def solution(mesh):
    def local(left_modes, right_modes, momenta, spin_perm, spin_phase):
        large = pl.BlockSpec(memory_space=pl.ANY)
        dma = pltpu.SemaphoreType.DMA
        return pl.pallas_call(
            kernel,
            out_shape=jax.ShapeDtypeStruct((2, MODES, MODES), FLOAT),
            in_specs=[large] * 5,
            out_specs=pl.BlockSpec(memory_space=pltpu.VMEM),
            scratch_shapes=[
                pltpu.SMEM((3, STRUCTS), jnp.int32),
                pltpu.SMEM((4, STRUCTS), jnp.int32),
                pltpu.SMEM((4, STRUCTS), jnp.int32),
                pltpu.VMEM((MODES, COMP, SITES), HALF),
                pltpu.VMEM((MODES, COMP, SITES), HALF),
                pltpu.VMEM((MODES * COMP, SITES), FLOAT),
                pltpu.VMEM((STRUCTS * 4, SITES), FLOAT),
                pltpu.VMEM((STRUCTS * 4, SITES), FLOAT),
                pltpu.VMEM((STRUCTS * 4, SITES), FLOAT),
                pltpu.VMEM((PAIRS, MODES, 2 * SITES), HALF),
                pltpu.VMEM((PAIRS, MODES, 2 * SITES), HALF),
                pltpu.VMEM((PAIRS, 2 * MODES, 2 * SITES), HALF),
                pltpu.VMEM((PAIRS, 2 * MODES, 2 * SITES), HALF),
                pltpu.VMEM((len(RELAYED), PER, MODES, 2 * SITES), HALF),
                pltpu.VMEM((2, 2, MODES, 2 * SITES), HALF),
                pltpu.VMEM((PAIRS, 2, STRUCTS, MODES, 2 * SITES), HALF),
                pltpu.VMEM((2, 2, STRUCTS, MODES, 2 * MODES), FLOAT),
                pltpu.VMEM((2, STRUCTS, 2, MODES, 2 * MODES), HALF),
                pltpu.VMEM((3, SLOTS, 2, MODES, 2 * MODES), HALF),
                pltpu.VMEM((3, 2, MODES, 2 * MODES), HALF),
                pltpu.VMEM((3, 2, MODES, 2 * MODES), HALF),
                dma((5,)),
                dma((PARTS,)),
                dma((PARTS,)),
                dma((len(RELAYED),)),
                dma((len(RELAYED),)),
                dma((len(LEFT_CUTS),)),
                dma((len(LEFT_CUTS),)),
                dma((2,)),
                dma((2,)),
                dma((2, STRUCTS)),
                dma((3, SLOTS)),
                dma((3, 2)),
                dma((3, 2)),
            ],
            compiler_params=pltpu.CompilerParams(
                collective_id=0, has_side_effects=True, vmem_limit_bytes=40 * 2**20
            ),
            cost_estimate=pl.CostEstimate(
                flops=2 * 1024 * 256 * 3072, bytes_accessed=2**20, transcendentals=8192
            ),
        )(
            *(
                pltpu.with_memory_space_constraint(array, pltpu.HBM)
                for array in (momenta.T, spin_perm.T, spin_phase.T, left_modes, right_modes)
            )
        )

    placed = (P("mode", None, "space"), P("mode", None, "space"), P(), P(), P())
    return jax.shard_map(
        local, mesh=mesh, in_specs=placed, out_specs=P("space", "mode", None), check_vma=False
    )
```
